128 devices in a mesh: tower: 16 (over z, y), dp: 8 (over x, core).
Axes of the slice: x: 4, y: 4, z: 4, core: 2. Of those that a mesh axis runs over, the one named last changes fastest.
Arguments:
- image_hidden: bfloat16 [16, 8, 128, 1664], P('tower', 'dp'), may hold values from -60 to 60
- text_hidden: bfloat16 [16, 8, 384, 1280], P('tower', 'dp'), may hold values from -60 to 60
- image_gain: float32 [1664], replicated, may hold values from 0.1 to 1.9
- text_gain: float32 [1280], replicated, may hold values from 0.1 to 1.9
- image_projection: bfloat16 [1664, 1280], replicated, may hold values from -0.1470871 to 4.147087
- text_projection: bfloat16 [1280, 1280], replicated, may hold values from -0.1677051 to 4.167705
- logit_scale: float32 [1], replicated, may hold values from 160 to 320
Outputs:
- image_grad: bfloat16 [16, 8, 128, 1664], P('tower', 'dp')
- text_grad: bfloat16 [16, 8, 384, 1280], P('tower', 'dp')
- mean_loss: float32 [1], replicated
The draws below stay inside these ranges and needn't reach their ends.
All inputs are finite; a program needn't handle non-finite values.
Results may differ from the reference program's by a relative error of at most 0.02.
Values may be sent and summed in bfloat16 or wider, within the bound.
No kernel may reach another device: no remote copies, remote signals or barrier semaphores. Data moves between devices by JAX's collectives and lax.ppermute only.
A program may use at most 192 MiB of HBM per device.

```python
import math
import jax
import jax.numpy as jnp
from jax import lax

DI = 1664
DT = 1280
DE = 1280
ROWS_DEV = 128
PAIRS = 12288
N_TOWER = 16
N_DP = 8


def pair_latent(key):
    strength_key, latent_key = jax.random.split(key)
    latent = jnp.clip(jax.random.normal(latent_key, (PAIRS, DE), jnp.float32), -6.0, 6.0)
    strength = jax.random.uniform(strength_key, (PAIRS, 1), jnp.float32)
    return (latent, strength)


def draw_image_hidden(key, part):
    latent, strength = pair_latent(key)
    key = jax.random.fold_in(key, 11)
    key_head, key_tail, key_spare = jax.random.split(key, 3)
    mixing = 0.9 * strength
    noise_head = jnp.clip(jax.random.normal(key_head, (PAIRS, DE), jnp.float32), -6.0, 6.0)
    head_rows = jnp.clip(mixing * latent + jnp.sqrt(1.0 - mixing * mixing) * noise_head, -6.0, 6.0)
    tail_rows = jnp.clip(jax.random.normal(key_tail, (PAIRS, DI - DE), jnp.float32), -6.0, 6.0)
    row_values = jnp.concatenate([head_rows, tail_rows], 1)
    groups = N_TOWER * 3 // 4
    used_blocks = row_values.reshape(groups, N_DP, ROWS_DEV, DI)
    spare_blocks = jnp.clip(jax.random.normal(key_spare, (N_TOWER - groups, N_DP, ROWS_DEV, DI), jnp.float32), -6.0, 6.0)
    return jnp.concatenate([used_blocks, spare_blocks], 0).astype(jnp.bfloat16)


def draw_text_hidden(key, part):
    latent, strength = pair_latent(key)
    key = jax.random.fold_in(key, 17)
    key_head, key_spare = jax.random.split(key, 2)
    mixing = 0.9 * strength
    noise_head = jnp.clip(jax.random.normal(key_head, (PAIRS, DT), jnp.float32), -6.0, 6.0)
    row_values = jnp.clip(mixing * latent + jnp.sqrt(1.0 - mixing * mixing) * noise_head, -6.0, 6.0)
    groups = N_TOWER * 3 // 4
    used_blocks = jnp.transpose(row_values.reshape(N_DP, N_TOWER - groups, 3 * ROWS_DEV, DT), (1, 0, 2, 3))
    spare_blocks = jnp.clip(jax.random.normal(key_spare, (groups, N_DP, 3 * ROWS_DEV, DT), jnp.float32), -6.0, 6.0)
    return jnp.concatenate([spare_blocks, used_blocks], 0).astype(jnp.bfloat16)


def draw_image_projection(key, part):
    key = jax.random.fold_in(key, 23)
    diagonal_boost = 2.0
    noise_part = jnp.clip(jax.random.normal(key, (DI, DE), jnp.float32), -6.0, 6.0) * DI ** (-0.5)
    identity = jnp.concatenate([jnp.eye(DE, dtype=jnp.float32), jnp.zeros((DI - DE, DE), jnp.float32)], 0)
    return (diagonal_boost * identity + noise_part).astype(jnp.bfloat16)


def draw_text_projection(key, part):
    key = jax.random.fold_in(key, 29)
    diagonal_boost = 2.0
    noise_part = jnp.clip(jax.random.normal(key, (DT, DE), jnp.float32), -6.0, 6.0) * DT ** (-0.5)
    return (diagonal_boost * jnp.eye(DT, DE, dtype=jnp.float32) + noise_part).astype(jnp.bfloat16)


def setup_inputs(seed: int = 0) -> dict:
    arg_keys = jax.random.split(jax.random.key(seed), 8)
    return {
        "image_hidden": draw_image_hidden(jax.random.fold_in(arg_keys[7], 71), 0),
        "text_hidden": draw_text_hidden(jax.random.fold_in(arg_keys[7], 71), 0),
        "image_gain": jnp.clip(1.0 + 0.18 * jax.random.normal(arg_keys[2], (DI,), jnp.float32), 0.1, 1.9),
        "text_gain": jnp.clip(1.0 + 0.18 * jax.random.normal(arg_keys[3], (DT,), jnp.float32), 0.1, 1.9),
        "image_projection": draw_image_projection(jax.random.fold_in(arg_keys[7], 71), 0),
        "text_projection": draw_text_projection(jax.random.fold_in(arg_keys[7], 71), 0),
        "logit_scale": jnp.clip(jnp.exp(jax.random.uniform(arg_keys[6], (1,), jnp.float32, math.log(160.0), math.log(320.0))), 160.0, 320.0),
    }


epsilon_norm = 1e-05
epsilon_unit = 1e-06

def forward_tower(row_values, gain, projection):
    values = row_values.astype(jnp.float32)
    centred = values - lax.optimization_barrier(jnp.mean(values, axis=1, keepdims=True))
    inverse = lax.rsqrt(lax.optimization_barrier(jnp.mean(centred * centred, axis=1, keepdims=True)) + epsilon_norm)
    normal_rows = centred * inverse
    normed = (normal_rows * gain).astype(jnp.bfloat16)
    projected = jnp.dot(normed, projection, preferred_element_type=jnp.float32)
    length = jnp.sqrt(lax.optimization_barrier(jnp.sum(projected * projected, axis=1, keepdims=True)) + epsilon_unit)
    unit_exact = projected / length
    return (unit_exact.astype(jnp.bfloat16), unit_exact, length, normal_rows, inverse)

def backward_tower(grad_unit, unit_exact, length, normal_rows, inverse, gain, projection):
    dot_along = lax.optimization_barrier(jnp.sum(unit_exact * grad_unit, axis=1, keepdims=True))
    grad_projected = ((grad_unit - unit_exact * dot_along) / length).astype(jnp.bfloat16)
    grad_normed = lax.dot_general(grad_projected, projection, (((1,), (1,)), ((), ())), preferred_element_type=jnp.float32)
    scaled = grad_normed * gain
    centre = lax.optimization_barrier(jnp.mean(scaled, axis=1, keepdims=True))
    tilt_mean = lax.optimization_barrier(jnp.mean(scaled * normal_rows, axis=1, keepdims=True))
    return (inverse * (scaled - centre - normal_rows * tilt_mean)).astype(jnp.bfloat16)

def log_sum_exp(logits):
    highest = lax.optimization_barrier(jnp.max(logits, axis=1))
    return highest + jnp.log(lax.optimization_barrier(jnp.sum(jnp.exp(logits - highest[:, None]), axis=1)))

def reference(image_hidden, text_hidden, image_gain, text_gain, image_projection, text_projection, logit_scale):
    groups = N_TOWER * 3 // 4
    image_rows = image_hidden[:groups].reshape(PAIRS, DI)
    text_rows = jnp.transpose(text_hidden[groups:], (1, 0, 2, 3)).reshape(PAIRS, DT)
    image_parts = forward_tower(image_rows, image_gain, image_projection)
    text_parts = forward_tower(text_rows, text_gain, text_projection)
    image_unit = image_parts[0]
    text_unit = text_parts[0]
    logit_mult = logit_scale[0]
    block_size = math.gcd(PAIRS, 1024)
    count_blocks = PAIRS // block_size

    def row_lse(block):
        return log_sum_exp(logit_mult * lax.dot_general(block, text_unit, (((1,), (1,)), ((), ())), preferred_element_type=jnp.float32))

    def col_lse(block):
        return log_sum_exp(logit_mult * lax.dot_general(block, image_unit, (((1,), (1,)), ((), ())), preferred_element_type=jnp.float32))
    row_values = lax.map(row_lse, image_unit.reshape(count_blocks, block_size, DE)).reshape(PAIRS)
    col_values = lax.map(col_lse, text_unit.reshape(count_blocks, block_size, DE)).reshape(PAIRS)
    diagonal = logit_mult * lax.optimization_barrier(jnp.sum(image_unit.astype(jnp.float32) * text_unit.astype(jnp.float32), axis=1))
    loss_value = (0.5 * (jnp.sum(row_values) + jnp.sum(col_values)) - jnp.sum(diagonal)) / PAIRS
    columns = jnp.arange(PAIRS, dtype=jnp.int32)

    def scan_step(running, inputs):
        block, block_lse, block_start = inputs
        logits = logit_mult * lax.dot_general(block, text_unit, (((1,), (1,)), ((), ())), preferred_element_type=jnp.float32)
        row_index = block_start + jnp.arange(block_size, dtype=jnp.int32)
        on_diagonal = row_index[:, None] == columns[None, :]
        softened = 0.5 * (jnp.exp(logits - block_lse[:, None]) + jnp.exp(logits - col_values[None, :]))
        grad_tile = (softened - on_diagonal.astype(jnp.float32)).astype(jnp.bfloat16)
        grad_rows = logit_mult * jnp.dot(grad_tile, text_unit, preferred_element_type=jnp.float32)
        running = running + logit_mult * lax.dot_general(grad_tile, block, (((0,), (0,)), ((), ())), preferred_element_type=jnp.float32)
        return (running, grad_rows)
    starts = jnp.arange(count_blocks, dtype=jnp.int32) * block_size
    text_grad_unit, image_grad_unit = lax.scan(scan_step, jnp.zeros((PAIRS, DE), jnp.float32), (image_unit.reshape(count_blocks, block_size, DE), row_values.reshape(count_blocks, block_size), starts))
    image_grad_unit = image_grad_unit.reshape(PAIRS, DE)
    image_back = backward_tower(image_grad_unit, image_parts[1], image_parts[2], image_parts[3], image_parts[4], image_gain, image_projection)
    text_back = backward_tower(text_grad_unit, text_parts[1], text_parts[2], text_parts[3], text_parts[4], text_gain, text_projection)
    image_out = image_back.reshape(groups, N_DP, ROWS_DEV, DI)
    image_out = jnp.concatenate([image_out, jnp.zeros((N_TOWER - groups, N_DP, ROWS_DEV, DI), jnp.bfloat16)], 0)
    text_out = jnp.transpose(text_back.reshape(N_DP, N_TOWER - groups, 3 * ROWS_DEV, DT), (1, 0, 2, 3))
    text_out = jnp.concatenate([jnp.zeros((groups, N_DP, 3 * ROWS_DEV, DT), jnp.bfloat16), text_out], 0)
    return (image_out, text_out, jnp.reshape(loss_value, (1,)))
```

```python
import jax
import jax.numpy as jnp
from jax import lax
from jax.sharding import PartitionSpec as P

bf = jnp.bfloat16
f32 = jnp.float32
epsilon_norm = 1e-05
epsilon_unit = 1e-06
lowest = -1e30
side = 4


def moved_z(a, step):
    pairs = [(z * 4 + y, (z + step) % 4 * 4 + y) for z in range(4) for y in range(4)]
    return lax.ppermute(a, "tower", pairs)


def moved_y(a, step):
    pairs = [(z * 4 + y, z * 4 + (y + step) % 4) for z in range(4) for y in range(4)]
    return lax.ppermute(a, "tower", pairs)


def moved_x(a, step):
    pairs = [(x * 2 + c, (x + step) % 4 * 2 + c) for x in range(4) for c in range(2)]
    return lax.ppermute(a, "dp", pairs)


def swapped(a, axis, bit):
    count = lax.axis_size(axis)
    return lax.ppermute(a, axis, [(i, i ^ bit) for i in range(count)])


def total(*terms):
    return sum(t.astype(f32) for t in terms).astype(bf)


def filled(parts, at):
    full = jnp.zeros((4,) + parts[0].shape, parts[0].dtype)
    for offset, part in parts.items():
        full = lax.dynamic_update_index_in_dim(full, part, (at + offset) % 4, 0)
    return full


def ring_gather(a, move, at):
    half = a.shape[0] // 2
    left = move(a, 1)
    right = move(a, -1)
    far = jnp.concatenate([move(left[:half], 1), move(right[half:], -1)], 0)
    return filled({0: a, 3: left, 1: right, 2: far}, at)


def direct_gather(a, move, at):
    return filled({0: a, 3: move(a, 1), 1: move(a, -1), 2: move(a, 2)}, at)


def ring_scatter(a, move, at):
    half = a.shape[1] // 2
    take = lambda offset: lax.dynamic_index_in_dim(a, (at + offset) % 4, 0, False)
    far = take(2)
    from_left = move(far[:half], 1)
    from_right = move(far[half:], -1)
    right = take(1)
    left = take(3)
    right = jnp.concatenate([total(right[:half], from_left), right[half:]], 0)
    left = jnp.concatenate([left[:half], total(left[half:], from_right)], 0)
    return total(take(0), move(right, 1), move(left, -1))


def direct_scatter(a, move, at):
    take = lambda offset: lax.dynamic_index_in_dim(a, (at + offset) % 4, 0, False)
    return total(take(0), move(take(1), 1), move(take(3), -1), move(take(2), 2))


def text_gather(a, z, y):
    half = a.shape[0] // 2
    one = ring_gather(direct_gather(a[:half], moved_z, z), moved_y, y)
    two = ring_gather(direct_gather(a[half:], moved_y, y), moved_z, z)
    width = a.shape[1]
    return jnp.concatenate([one.reshape(-1, width), two.reshape(-1, width)], 0)


def text_scatter(a, z, y):
    width = a.shape[1]
    parts = a.reshape(2, 4, 4, -1, width)
    one = direct_scatter(ring_scatter(parts[0], moved_y, y), moved_z, z)
    two = direct_scatter(ring_scatter(parts[1], moved_z, z), moved_y, y)
    return jnp.concatenate([one, two], 0)


def image_gather(a, x, c):
    mine = ring_gather(a, moved_x, x)
    other = swapped(mine, "dp", 1)
    low = jnp.where(c == 0, mine, other)
    high = jnp.where(c == 0, other, mine)
    return jnp.stack([low, high], 1).reshape(-1, a.shape[1])


def image_scatter(a, x, c):
    width = a.shape[1]
    parts = a.reshape(4, 2, -1, width)
    take = lambda i: lax.dynamic_index_in_dim(parts, i, 1, False)
    got = swapped(take(1 - c), "dp", 1)
    return ring_scatter(total(take(c), got), moved_x, x)


def spread(rows, z, y):
    count = rows.shape[0] // 4
    own = jnp.where(z == 3, rows[3 * count :], jnp.zeros_like(rows[:count]))
    for q in range(3):
        pairs = [(12 + k, q * 4 + k) for k in range(4)]
        own = own + lax.ppermute(rows[q * count : (q + 1) * count], "tower", pairs)
    return own


def collected(part, z, y):
    got = [lax.ppermute(part, "tower", [(q * 4 + k, 12 + k) for k in range(4)]) for q in range(3)]
    return jnp.concatenate(got + [jnp.where(z == 3, part, jnp.zeros_like(part))], 0)


def merged(row, col):
    for k in range(4):
        if k < 3:
            row = jnp.logaddexp(row, swapped(row, "dp", 1 << k))
        col = jnp.logaddexp(col, swapped(col, "tower", 1 << k))
    return row, col


def summed(value):
    for k in range(3):
        value = value + swapped(value, "dp", 1 << k)
    for k in range(4):
        value = value + swapped(value, "tower", 1 << k)
    return value


def forward_tower(row_values, gain, projection):
    values = row_values.astype(f32)
    centred = values - jnp.mean(values, axis=1, keepdims=True)
    inverse = lax.rsqrt(jnp.mean(centred * centred, axis=1, keepdims=True) + epsilon_norm)
    normal_rows = centred * inverse
    normed = (normal_rows * gain).astype(bf)
    projected = jnp.dot(normed, projection, preferred_element_type=f32)
    length = jnp.sqrt(jnp.sum(projected * projected, axis=1, keepdims=True) + epsilon_unit)
    unit_exact = projected / length
    return (unit_exact.astype(bf), unit_exact, length, normal_rows, inverse)


def backward_tower(grad_unit, unit_exact, length, normal_rows, inverse, gain, projection):
    dot_along = jnp.sum(unit_exact * grad_unit, axis=1, keepdims=True)
    grad_projected = ((grad_unit - unit_exact * dot_along) / length).astype(bf)
    grad_normed = lax.dot_general(
        grad_projected, projection, (((1,), (1,)), ((), ())), preferred_element_type=f32
    )
    scaled = grad_normed * gain
    centre = jnp.mean(scaled, axis=1, keepdims=True)
    tilt_mean = jnp.mean(scaled * normal_rows, axis=1, keepdims=True)
    return (inverse * (scaled - centre - normal_rows * tilt_mean)).astype(bf)


def local(
    image_hidden, text_hidden, image_gain, text_gain, image_projection, text_projection, logit_scale
):
    tower_at = lax.axis_index("tower")
    lane_at = lax.axis_index("dp")
    z, y, x, c = tower_at // 4, tower_at % 4, lane_at // 2, lane_at % 2
    is_image = z < 3
    image_rows = image_hidden[0, 0]
    text_rows = spread(text_hidden[0, 0], z, y)
    rows_dev = image_rows.shape[0]
    text_dev = text_rows.shape[0]
    logit_mult = logit_scale[0]
    text_parts = forward_tower(text_rows, text_gain, text_projection)
    image_parts = forward_tower(image_rows, image_gain, image_projection)
    text_block = text_gather(text_parts[0], z, y)
    image_unit = jnp.where(is_image, image_parts[0], jnp.zeros_like(image_parts[0]))
    image_block = image_gather(image_unit, x, c)
    block_rows = image_block.shape[0]
    block_cols = text_block.shape[0]
    pair_count = block_rows * 12
    part = text_dev // 2
    place = jnp.arange(block_cols, dtype=jnp.int32)
    later = place // (block_cols // 2)
    slow = place // (4 * part) % 4
    fast = place // part % 4
    col_y = jnp.where(later == 0, slow, fast)
    col_z = jnp.where(later == 0, fast, slow)
    col_index = lane_at * block_cols + col_y * (4 * text_dev) + col_z * text_dev + later * part + place % part
    row_index = tower_at * block_rows + jnp.arange(block_rows, dtype=jnp.int32)
    on_diagonal = row_index[:, None] == col_index[None, :]

    logits = logit_mult * lax.dot_general(
        image_block, text_block, (((1,), (1,)), ((), ())), preferred_element_type=f32
    ) + jnp.where(is_image, 0.0, lowest)
    row_high = jnp.max(logits, axis=1)
    row_part = row_high + jnp.log(jnp.sum(jnp.exp(logits - row_high[:, None]), axis=1))
    col_high = jnp.max(logits, axis=0)
    col_part = col_high + jnp.log(jnp.sum(jnp.exp(logits - col_high[None, :]), axis=0))
    row_lse, col_lse = merged(row_part, col_part)

    softened = 0.5 * (jnp.exp(logits - row_lse[:, None]) + jnp.exp(logits - col_lse[None, :]))
    grad_tile = (softened - on_diagonal.astype(f32)).astype(bf)
    text_partial = (
        logit_mult
        * lax.dot_general(grad_tile, image_block, (((0,), (0,)), ((), ())), preferred_element_type=f32)
    ).astype(bf)
    text_sum = text_scatter(text_partial, z, y).astype(f32)
    image_partial = (
        logit_mult * jnp.dot(grad_tile, text_block, preferred_element_type=f32)
    ).astype(bf)
    image_sum = image_scatter(image_partial, x, c).astype(f32)

    matched = jnp.sum(jnp.where(on_diagonal, logits, 0.0))
    own_rows = lax.dynamic_slice_in_dim(row_lse, lane_at * rows_dev, rows_dev, 0)
    first = lax.dynamic_slice_in_dim(col_lse, (y * 4 + z) * part, part, 0)
    second = lax.dynamic_slice_in_dim(col_lse, block_cols // 2 + (z * 4 + y) * part, part, 0)
    of_rows = jnp.where(is_image, 0.5 * jnp.sum(own_rows) - matched, 0.0)
    loss_piece = of_rows + 0.5 * (jnp.sum(first) + jnp.sum(second))
    loss_value = summed(jnp.reshape(loss_piece, (1,))) / pair_count

    text_out = collected(backward_tower(text_sum, *text_parts[1:], text_gain, text_projection), z, y)
    image_out = backward_tower(image_sum, *image_parts[1:], image_gain, image_projection)
    image_out = jnp.where(is_image, image_out, jnp.zeros_like(image_out))
    return (image_out[None, None], text_out[None, None], loss_value)


def solution(mesh):
    in_specs = (P("tower", "dp", None, None), P("tower", "dp", None, None), P(), P(), P(), P(), P())
    out_specs = (P("tower", "dp", None, None), P("tower", "dp", None, None), P())
    return jax.shard_map(local, mesh=mesh, in_specs=in_specs, out_specs=out_specs, check_vma=False)
```

```python
import jax
import jax.numpy as jnp
from jax import lax
from jax.sharding import PartitionSpec as P

bf = jnp.bfloat16
f32 = jnp.float32
epsilon_norm = 1e-05
epsilon_unit = 1e-06
lowest = -1e30


def moved_z(a, step):
    pairs = [(z * 4 + y, (z + step) % 4 * 4 + y) for z in range(4) for y in range(4)]
    return lax.ppermute(a, "tower", pairs)


def moved_y(a, step):
    pairs = [(z * 4 + y, z * 4 + (y + step) % 4) for z in range(4) for y in range(4)]
    return lax.ppermute(a, "tower", pairs)


def moved_x(a, step):
    pairs = [(x * 2 + c, (x + step) % 4 * 2 + c) for x in range(4) for c in range(2)]
    return lax.ppermute(a, "dp", pairs)


def swapped(a, axis, bit):
    count = lax.axis_size(axis)
    return lax.ppermute(a, axis, [(i, i ^ bit) for i in range(count)])


def total(*terms):
    return sum(t.astype(f32) for t in terms).astype(bf)


def after(value, *earlier):
    return lax.optimization_barrier((value, *earlier))[0]


def near_far(a, move):
    return {0: a, 1: move(a, -1), 3: move(a, 1), 2: move(a, 2)}


def in_order(parts):
    return jnp.concatenate([parts[k] for k in range(4)], 0)


def ring_gather(a, move):
    half = a.shape[0] // 2
    left = move(a, 1)
    right = move(a, -1)
    far = jnp.concatenate([move(left[:half], 1), move(right[half:], -1)], 0)
    return {0: a, 1: right, 3: left, 2: far}


def ring_near(parts, move):
    far = parts[2]
    half = far.shape[0] // 2
    from_left = move(far[:half], 1)
    from_right = move(far[half:], -1)
    right = jnp.concatenate([total(parts[1][:half], from_left), parts[1][half:]], 0)
    left = jnp.concatenate([parts[3][:half], total(parts[3][half:], from_right)], 0)
    return right, left


def ring_end(own, right, left, move):
    return total(own, move(right, 1), move(left, -1))


def direct_scatter(a, move):
    count = a.shape[0] // 4
    take = lambda k: a[k * count : (k + 1) * count]
    return total(take(0), move(take(1), 1), move(take(3), -1), move(take(2), 2))


def spread(rows, z, y):
    count = rows.shape[0] // 4
    own = jnp.where(z == 3, rows[3 * count :], jnp.zeros_like(rows[:count]))
    for q in range(3):
        pairs = [(12 + k, q * 4 + k) for k in range(4)]
        own = own + lax.ppermute(rows[q * count : (q + 1) * count], "tower", pairs)
    return own


def collected(part, z, y):
    got = [lax.ppermute(part, "tower", [(q * 4 + k, 12 + k) for k in range(4)]) for q in range(3)]
    return jnp.concatenate(got + [jnp.where(z == 3, part, jnp.zeros_like(part))], 0)


def joined(parts):
    highest = parts[0]
    for part in parts[1:]:
        highest = jnp.maximum(highest, part)
    return highest + jnp.log(sum(jnp.exp(part - highest) for part in parts))


def turned(a, step, blocks):
    turned_rows = lambda h: jnp.concatenate([h[4 - step :], h[: 4 - step]], 0)
    cut = a.shape[1] - a.shape[1] // 4 * step
    turned_part = lambda h: jnp.concatenate([h[:, cut:], h[:, :cut]], 1)
    halves = [a[:4], a[4:]]
    return jnp.concatenate(
        [turned_rows(h) if by_block else turned_part(h) for h, by_block in zip(halves, blocks)], 0
    )


def exchanged(a, move, blocks):
    got = {s: turned(move(a, -s), s, blocks) for s in (1, 3, 2)}
    return joined([a, got[1], got[2], got[3]])


def forward_tower(row_values, gain, projection):
    values = row_values.astype(f32)
    centred = values - jnp.mean(values, axis=1, keepdims=True)
    inverse = lax.rsqrt(jnp.mean(centred * centred, axis=1, keepdims=True) + epsilon_norm)
    normal_rows = centred * inverse
    normed = (normal_rows * gain).astype(bf)
    projected = jnp.dot(normed, projection, preferred_element_type=f32)
    length = jnp.sqrt(jnp.sum(projected * projected, axis=1, keepdims=True) + epsilon_unit)
    unit_exact = projected / length
    return (unit_exact.astype(bf), unit_exact, length, normal_rows, inverse)


def backward_tower(grad_unit, unit_exact, length, normal_rows, inverse, gain, projection):
    dot_along = jnp.sum(unit_exact * grad_unit, axis=1, keepdims=True)
    grad_projected = ((grad_unit - unit_exact * dot_along) / length).astype(bf)
    grad_normed = lax.dot_general(
        grad_projected, projection, (((1,), (1,)), ((), ())), preferred_element_type=f32
    )
    scaled = grad_normed * gain
    centre = jnp.mean(scaled, axis=1, keepdims=True)
    tilt_mean = jnp.mean(scaled * normal_rows, axis=1, keepdims=True)
    return (inverse * (scaled - centre - normal_rows * tilt_mean)).astype(bf)


def local(
    image_hidden, text_hidden, image_gain, text_gain, image_projection, text_projection, logit_scale
):
    tower_at = lax.axis_index("tower")
    lane_at = lax.axis_index("dp")
    z, y, x, c = tower_at // 4, tower_at % 4, lane_at // 2, lane_at % 2
    is_image = z < 3
    image_rows = image_hidden[0, 0]
    text_rows = spread(text_hidden[0, 0], z, y)
    rows_dev = image_rows.shape[0]
    text_dev = text_rows.shape[0]
    width = image_projection.shape[1]
    part = text_dev // 2
    block = 4 * part
    logit_mult = logit_scale[0]
    image_parts = forward_tower(image_rows, image_gain, image_projection)
    text_parts = forward_tower(text_rows, text_gain, text_projection)

    text_unit = text_parts[0]
    one_own = in_order(near_far(text_unit[:part], moved_z))
    two_own = in_order(near_far(text_unit[part:], moved_y))
    image_unit = jnp.where(is_image, image_parts[0], jnp.zeros_like(image_parts[0]))
    image_unit = after(image_unit, text_unit)
    mine = in_order(near_far(image_unit, moved_x))
    other = swapped(mine, "dp", 1)
    one = ring_gather(one_own, moved_y)
    two = ring_gather(two_own, moved_z)
    image_block = jnp.concatenate([mine, other], 0)
    text_block = jnp.concatenate(
        [one[2], two[2], one[1], one[3], two[1], two[3], one[0], two[0]], 0
    )
    block_rows = image_block.shape[0]
    block_cols = text_block.shape[0]
    pair_count = block_rows * 12

    steps = jnp.arange(4, dtype=jnp.int32)
    lanes = jnp.concatenate([2 * ((x + steps) % 4) + c, 2 * ((x + steps) % 4) + 1 - c])
    row_index = (
        tower_at * block_rows + lanes[:, None] * rows_dev + jnp.arange(rows_dev, dtype=jnp.int32)
    ).reshape(-1)
    inside = jnp.arange(part, dtype=jnp.int32)
    row_of = (y + steps) % 4 * (4 * text_dev)
    plane_of = (z + steps) % 4 * text_dev
    one_index = row_of[:, None, None] + plane_of[None, :, None] + inside
    two_index = plane_of[:, None, None] + row_of[None, :, None] + part + inside
    index = jnp.concatenate([one_index, two_index], 0).reshape(8, block)
    col_index = lane_at * block_cols + index[jnp.array([2, 6, 1, 3, 5, 7, 0, 4])].reshape(-1)
    on_diagonal = row_index[:, None] == col_index[None, :]

    logits = logit_mult * lax.dot_general(
        image_block, text_block, (((1,), (1,)), ((), ())), preferred_element_type=f32
    ) + jnp.where(is_image, 0.0, lowest)
    row_high = jnp.max(logits, axis=1)
    row_part = row_high + jnp.log(jnp.sum(jnp.exp(logits - row_high[:, None]), axis=1))
    col_high = jnp.max(logits, axis=0)
    col_part = col_high + jnp.log(jnp.sum(jnp.exp(logits - col_high[None, :]), axis=0))
    row_stat = row_part.reshape(8, rows_dev)
    col_stat = col_part.reshape(8, block)
    col_stat = jnp.concatenate([col_stat[k][None] for k in (6, 2, 0, 3, 7, 4, 1, 5)], 0)
    col_stat = exchanged(col_stat, moved_z, (False, True))
    row_stat = exchanged(row_stat, moved_x, (True, True))
    col_stat = exchanged(col_stat, moved_y, (True, False))
    got = swapped(row_stat, "dp", 1)
    row_stat = joined([row_stat, jnp.concatenate([got[4:], got[:4]], 0)])
    row_lse = row_stat.reshape(-1)
    col_lse = jnp.concatenate([col_stat[k][None] for k in (2, 6, 1, 3, 5, 7, 0, 4)], 0).reshape(-1)

    softened = 0.5 * (jnp.exp(logits - row_lse[:, None]) + jnp.exp(logits - col_lse[None, :]))
    grad_tile = (softened - on_diagonal.astype(f32)).astype(bf)
    text_partial = (
        logit_mult
        * lax.dot_general(grad_tile, image_block, (((0,), (0,)), ((), ())), preferred_element_type=f32)
    ).astype(bf)
    take = lambda i: text_partial[i * block : (i + 1) * block]
    one_near = ring_near({2: take(0), 1: take(2), 3: take(3)}, moved_y)
    two_near = ring_near({2: take(1), 1: take(4), 3: take(5)}, moved_z)
    image_partial = (
        logit_mult * jnp.dot(grad_tile, text_block, preferred_element_type=f32)
    ).astype(bf)
    one_sum = ring_end(take(6), *one_near, moved_y)
    two_sum = ring_end(take(7), *two_near, moved_z)
    image_pair = total(image_partial[: 4 * rows_dev], swapped(image_partial[4 * rows_dev :], "dp", 1))
    image_sum = direct_scatter(image_pair, moved_x).astype(f32)
    one_last = direct_scatter(one_sum, moved_z)
    two_last = direct_scatter(two_sum, moved_y)
    text_sum = jnp.concatenate([one_last, two_last], 0).astype(f32)

    matched = jnp.sum(jnp.where(on_diagonal, logits, 0.0))
    of_rows = jnp.where(is_image, 0.5 * jnp.sum(row_stat[0]) - matched, 0.0)
    loss_piece = of_rows + 0.5 * (jnp.sum(col_stat[0, :part]) + jnp.sum(col_stat[4, :part]))
    loss = after(jnp.reshape(loss_piece, (1,)), one_near[0], two_near[0])
    for k in range(3):
        loss = loss + swapped(loss, "dp", 1 << k)
    loss = after(loss, one_sum, two_sum)
    for k in range(4):
        loss = loss + swapped(loss, "tower", 1 << k)
    loss_value = loss / pair_count

    image_out = backward_tower(image_sum, *image_parts[1:], image_gain, image_projection)
    image_out = jnp.where(is_image, image_out, jnp.zeros_like(image_out))
    text_out = collected(backward_tower(text_sum, *text_parts[1:], text_gain, text_projection), z, y)
    return (image_out[None, None], text_out[None, None], loss_value)


def solution(mesh):
    in_specs = (P("tower", "dp", None, None), P("tower", "dp", None, None), P(), P(), P(), P(), P())
    out_specs = (P("tower", "dp", None, None), P("tower", "dp", None, None), P())
    return jax.shard_map(local, mesh=mesh, in_specs=in_specs, out_specs=out_specs, check_vma=False)
```

```python
import jax
import jax.numpy as jnp
from jax import lax
from jax.sharding import PartitionSpec as P

bf = jnp.bfloat16
f32 = jnp.float32
epsilon_norm = 1e-05
epsilon_unit = 1e-06
lowest = -1e30
note_rows = 16


def moved_z(a, step):
    pairs = [(z * 4 + y, (z + step) % 4 * 4 + y) for z in range(4) for y in range(4)]
    return lax.ppermute(a, "tower", pairs)


def moved_y(a, step):
    pairs = [(z * 4 + y, z * 4 + (y + step) % 4) for z in range(4) for y in range(4)]
    return lax.ppermute(a, "tower", pairs)


def moved_x(a, step):
    pairs = [(x * 2 + c, (x + step) % 4 * 2 + c) for x in range(4) for c in range(2)]
    return lax.ppermute(a, "dp", pairs)


def swapped(a, axis, bit):
    count = lax.axis_size(axis)
    return lax.ppermute(a, axis, [(i, i ^ bit) for i in range(count)])


def total(*terms):
    return sum(t.astype(f32) for t in terms).astype(bf)


def after(value, *earlier):
    return lax.optimization_barrier((value, *earlier))[0]


def near_far(a, move):
    return {0: a, 1: move(a, -1), 3: move(a, 1), 2: move(a, 2)}


def in_order(parts):
    return jnp.concatenate([parts[k] for k in range(4)], 0)


def ring_gather(a, move):
    half = a.shape[0] // 2
    left = move(a, 1)
    right = move(a, -1)
    far = jnp.concatenate([move(left[:half], 1), move(right[half:], -1)], 0)
    return {0: a, 1: right, 3: left, 2: far}


def noted(block, value):
    high = lax.reduce_precision(value, 8, 7)
    middle = lax.reduce_precision(value - high, 8, 7)
    low = value - high - middle
    lane = lax.broadcasted_iota(jnp.int32, (note_rows, block.shape[1]), 1)
    terms = jnp.where(lane == 0, high, jnp.where(lane == 1, middle, jnp.where(lane == 2, low, 0.0)))
    return jnp.concatenate([block, terms.astype(bf)], 0)


def read(block):
    count = block.shape[0] - note_rows
    return block[:count], jnp.sum(block[count, :3].astype(f32))


def sent_read(block, value, move, step):
    return read(move(noted(block, value), step))


def ring_sum(values):
    return (values[0] + values[2]) + (values[1] + values[3])


def direct_scatter(a, value, move):
    count = a.shape[0] // 4
    take = lambda k: a[k * count : (k + 1) * count]
    left, right, far = [sent_read(take(k), value, move, k) for k in (1, 3, 2)]
    parts = [take(0), left[0], right[0], far[0]]
    return parts, ring_sum({0: value, 1: right[1], 2: far[1], 3: left[1]})


def spread(rows, z, y):
    count = rows.shape[0] // 4
    own = jnp.where(z == 3, rows[3 * count :], jnp.zeros_like(rows[:count]))
    for q in range(3):
        pairs = [(12 + k, q * 4 + k) for k in range(4)]
        own = own + lax.ppermute(rows[q * count : (q + 1) * count], "tower", pairs)
    return own


def collected(part, z, y):
    got = [lax.ppermute(part, "tower", [(q * 4 + k, 12 + k) for k in range(4)]) for q in range(3)]
    return jnp.concatenate(got + [jnp.where(z == 3, part, jnp.zeros_like(part))], 0)


def joined(parts):
    highest = parts[0]
    for part in parts[1:]:
        highest = jnp.maximum(highest, part)
    terms = [jnp.exp(part - highest) for part in parts]
    return highest + jnp.log(ring_sum(terms) if len(terms) == 4 else terms[0] + terms[1])


def turned(a, step, blocks):
    turned_rows = lambda h: jnp.concatenate([h[4 - step :], h[: 4 - step]], 0)
    cut = a.shape[1] - a.shape[1] // 4 * step
    turned_part = lambda h: jnp.concatenate([h[:, cut:], h[:, :cut]], 1)
    halves = [a[:4], a[4:]]
    return jnp.concatenate(
        [turned_rows(h) if by_block else turned_part(h) for h, by_block in zip(halves, blocks)], 0
    )


def exchanged(a, move, blocks):
    got = {s: turned(move(a, -s), s, blocks) for s in (1, 3, 2)}
    return joined([a, got[1], got[2], got[3]])


def exchanged_with_sum(a, extra, move, blocks):
    held = jnp.concatenate([a, extra], 0)
    got = {s: move(held, -s) for s in (1, 3, 2)}
    return (
        joined([a] + [turned(got[s][:8], s, blocks) for s in (1, 2, 3)]),
        ring_sum({k: (extra if k == 0 else got[k][8:])[0, 0] for k in range(4)}),
    )


def forward_tower(row_values, gain, projection):
    values = row_values.astype(f32)
    centred = values - jnp.mean(values, axis=1, keepdims=True)
    inverse = lax.rsqrt(jnp.mean(centred * centred, axis=1, keepdims=True) + epsilon_norm)
    normal_rows = centred * inverse
    normed = (normal_rows * gain).astype(bf)
    projected = jnp.dot(normed, projection, preferred_element_type=f32)
    length = jnp.sqrt(jnp.sum(projected * projected, axis=1, keepdims=True) + epsilon_unit)
    unit_exact = projected / length
    return (unit_exact.astype(bf), unit_exact, length, normal_rows, inverse)


def backward_tower(grad_unit, unit_exact, length, normal_rows, inverse, gain, projection):
    dot_along = jnp.sum(unit_exact * grad_unit, axis=1, keepdims=True)
    grad_projected = ((grad_unit - unit_exact * dot_along) / length).astype(bf)
    grad_normed = lax.dot_general(
        grad_projected, projection, (((1,), (1,)), ((), ())), preferred_element_type=f32
    )
    scaled = grad_normed * gain
    centre = jnp.mean(scaled, axis=1, keepdims=True)
    tilt_mean = jnp.mean(scaled * normal_rows, axis=1, keepdims=True)
    return (inverse * (scaled - centre - normal_rows * tilt_mean)).astype(bf)


def local(
    image_hidden, text_hidden, image_gain, text_gain, image_projection, text_projection, logit_scale
):
    tower_at = lax.axis_index("tower")
    lane_at = lax.axis_index("dp")
    z, y, x, c = tower_at // 4, tower_at % 4, lane_at // 2, lane_at % 2
    is_image = z < 3
    image_rows = image_hidden[0, 0]
    text_rows = spread(text_hidden[0, 0], z, y)
    rows_dev = image_rows.shape[0]
    text_dev = text_rows.shape[0]
    width = image_projection.shape[1]
    part = text_dev // 2
    block = 4 * part
    logit_mult = logit_scale[0]
    image_parts = forward_tower(image_rows, image_gain, image_projection)
    text_rows = after(text_rows, image_parts[0])
    text_parts = forward_tower(text_rows, text_gain, text_projection)

    text_unit = text_parts[0]
    one_own = in_order(near_far(text_unit[:part], moved_z))
    two_own = in_order(near_far(text_unit[part:], moved_y))
    image_unit = jnp.where(is_image, image_parts[0], jnp.zeros_like(image_parts[0]))
    image_near = near_far(image_unit, moved_x)
    mine = in_order(after(image_near, one_own, two_own))
    other = swapped(mine, "dp", 1)
    one = ring_gather(one_own, moved_y)
    two = ring_gather(two_own, moved_z)
    image_block = jnp.concatenate([mine, other], 0)
    text_block = jnp.concatenate(
        [one[2], two[2], one[1], one[3], two[1], two[3], one[0], two[0]], 0
    )
    block_rows = image_block.shape[0]
    block_cols = text_block.shape[0]
    pair_count = block_rows * 12

    steps = jnp.arange(4, dtype=jnp.int32)
    lanes = jnp.concatenate([2 * ((x + steps) % 4) + c, 2 * ((x + steps) % 4) + 1 - c])
    row_index = (
        tower_at * block_rows + lanes[:, None] * rows_dev + jnp.arange(rows_dev, dtype=jnp.int32)
    ).reshape(-1)
    inside = jnp.arange(part, dtype=jnp.int32)
    row_of = (y + steps) % 4 * (4 * text_dev)
    plane_of = (z + steps) % 4 * text_dev
    one_index = row_of[:, None, None] + plane_of[None, :, None] + inside
    two_index = plane_of[:, None, None] + row_of[None, :, None] + part + inside
    index = jnp.concatenate([one_index, two_index], 0).reshape(8, block)
    col_index = lane_at * block_cols + index[jnp.array([2, 6, 1, 3, 5, 7, 0, 4])].reshape(-1)
    on_diagonal = row_index[:, None] == col_index[None, :]

    logits = logit_mult * lax.dot_general(
        image_block, text_block, (((1,), (1,)), ((), ())), preferred_element_type=f32
    ) + jnp.where(is_image, 0.0, lowest)
    row_high = jnp.max(logits, axis=1)
    row_part = row_high + jnp.log(jnp.sum(jnp.exp(logits - row_high[:, None]), axis=1))
    col_high = jnp.max(logits, axis=0)
    col_part = col_high + jnp.log(jnp.sum(jnp.exp(logits - col_high[None, :]), axis=0))
    matched = jnp.sum(jnp.where(on_diagonal, logits, 0.0))
    row_stat = row_part.reshape(8, rows_dev)
    col_stat = col_part.reshape(8, block)
    col_stat = jnp.concatenate([col_stat[k][None] for k in (6, 2, 0, 3, 7, 4, 1, 5)], 0)
    col_stat = exchanged(col_stat, moved_z, (False, True))
    extra = jnp.full((8, rows_dev), matched, f32)
    row_stat, matched = exchanged_with_sum(row_stat, extra, moved_x, (True, True))
    extra = jnp.full((8, rows_dev), matched, f32)
    col_stat = exchanged(col_stat, moved_y, (True, False))
    got = swapped(jnp.concatenate([row_stat, extra], 0), "dp", 1)
    row_stat = joined([row_stat, jnp.concatenate([got[4:8], got[:4]], 0)])
    matched_all = matched + got[8, 0]
    row_lse = row_stat.reshape(-1)
    col_lse = jnp.concatenate([col_stat[k][None] for k in (2, 6, 1, 3, 5, 7, 0, 4)], 0).reshape(-1)

    row_sums = jnp.sum(row_stat, axis=1)
    same = ring_sum({k: row_sums[k] for k in range(4)})
    partner = ring_sum({k: row_sums[4 + k] for k in range(4)})
    of_rows = same + partner
    of_tower = jnp.where(is_image, 0.5 * of_rows - matched_all, 0.0)
    col_sums = jnp.sum(col_stat.reshape(8, 4, part), axis=2)
    one_sums = {k: ring_sum({j: col_sums[k, j] for j in range(4)}) for k in range(4)}
    two_sums = {k: ring_sum({j: col_sums[4 + k, j] for j in range(4)}) for k in range(4)}
    of_lane = 0.5 * (ring_sum(one_sums) + ring_sum(two_sums))
    softened = 0.5 * (jnp.exp(logits - row_lse[:, None]) + jnp.exp(logits - col_lse[None, :]))
    grad_tile = (softened - on_diagonal.astype(f32)).astype(bf)
    text_partial = (
        logit_mult
        * lax.dot_general(grad_tile, image_block, (((0,), (0,)), ((), ())), preferred_element_type=f32)
    ).astype(bf)
    take = lambda i: text_partial[i * block : (i + 1) * block]
    half = block // 2
    one_left = sent_read(take(0)[:half], of_tower, moved_y, 1)
    one_right = sent_read(take(0)[half:], of_tower, moved_y, -1)
    two_left = moved_z(take(1)[:half], 1)
    two_right = moved_z(take(1)[half:], -1)
    image_other = (
        logit_mult * jnp.dot(grad_tile[4 * rows_dev :], text_block, preferred_element_type=f32)
    ).astype(bf)
    one_left, one_right, two_left, two_right, image_other = lax.optimization_barrier(
        (one_left, one_right, two_left, two_right, image_other)
    )
    one_to_right = jnp.concatenate([total(take(2)[:half], one_left[0]), take(2)[half:]], 0)
    one_to_left = jnp.concatenate([take(3)[:half], total(take(3)[half:], one_right[0])], 0)
    two_to_right = jnp.concatenate([total(take(4)[:half], two_left), take(4)[half:]], 0)
    two_to_left = jnp.concatenate([take(5)[:half], total(take(5)[half:], two_right)], 0)
    one_to_right = noted(one_to_right, one_left[1])
    one_to_right, one_to_left, two_to_right, two_to_left, grad_mine = lax.optimization_barrier(
        (one_to_right, one_to_left, two_to_right, two_to_left, grad_tile[: 4 * rows_dev])
    )
    one_in_left = read(moved_y(one_to_right, 1))
    one_in_right = moved_y(one_to_left, -1)
    two_in_left = moved_z(two_to_right, 1)
    two_in_right = moved_z(two_to_left, -1)
    other_in, lane_in = read(swapped(noted(image_other, of_lane), "dp", 1))
    image_mine = (
        logit_mult * jnp.dot(grad_mine, text_block, preferred_element_type=f32)
    ).astype(bf)
    image_pair = total(image_mine, other_in)
    one_in_left, one_in_right, two_in_left, two_in_right, image_pair = lax.optimization_barrier(
        (one_in_left, one_in_right, two_in_left, two_in_right, image_pair)
    )
    image_terms, of_lane = direct_scatter(image_pair, of_lane + lane_in, moved_x)
    one_sum = total(take(6), one_in_left[0], one_in_right)
    two_sum = total(take(7), two_in_left, two_in_right)
    of_tower = ring_sum({0: of_tower, 1: one_right[1], 2: one_in_left[1], 3: one_left[1]})
    one_sum, two_sum, image_terms = lax.optimization_barrier((one_sum, two_sum, image_terms))
    one_terms, of_tower = direct_scatter(one_sum, of_tower, moved_z)
    two_take = lambda k: two_sum[k * part : (k + 1) * part]
    two_terms = [two_take(0)] + [moved_y(two_take(k), k) for k in (1, 3, 2)]
    image_sum = total(*image_terms).astype(f32)
    loss_value = jnp.reshape(of_tower + of_lane, (1,)) / pair_count

    image_out = backward_tower(image_sum, *image_parts[1:], image_gain, image_projection)
    image_out = jnp.where(is_image, image_out, jnp.zeros_like(image_out))
    one_terms, two_terms = after((one_terms, two_terms), image_out)
    text_sum = jnp.concatenate([total(*one_terms), total(*two_terms)], 0).astype(f32)
    text_out = collected(backward_tower(text_sum, *text_parts[1:], text_gain, text_projection), z, y)
    return (image_out[None, None], text_out[None, None], loss_value)


def solution(mesh):
    in_specs = (P("tower", "dp", None, None), P("tower", "dp", None, None), P(), P(), P(), P(), P())
    out_specs = (P("tower", "dp", None, None), P("tower", "dp", None, None), P())
    return jax.shard_map(local, mesh=mesh, in_specs=in_specs, out_specs=out_specs, check_vma=False)
```

```python
import functools

import jax
import jax.numpy as jnp
import numpy as np
from jax import lax
from jax.experimental import pallas as pl
from jax.experimental.pallas import tpu as pltpu
from jax.sharding import PartitionSpec as P

bf = jnp.bfloat16
f32 = jnp.float32
epsilon_norm = 1e-05
epsilon_unit = 1e-06
lowest = -1e30


def moved_z(a, step):
    pairs = [(z * 4 + y, (z + step) % 4 * 4 + y) for z in range(4) for y in range(4)]
    return lax.ppermute(a, "tower", pairs)


def moved_y(a, step):
    pairs = [(z * 4 + y, z * 4 + (y + step) % 4) for z in range(4) for y in range(4)]
    return lax.ppermute(a, "tower", pairs)


def moved_x(a, step):
    pairs = [(x * 2 + c, (x + step) % 4 * 2 + c) for x in range(4) for c in range(2)]
    return lax.ppermute(a, "dp", pairs)


def swapped(a, axis, bit):
    count = lax.axis_size(axis)
    return lax.ppermute(a, axis, [(i, i ^ bit) for i in range(count)])


def after(value, *earlier):
    return lax.optimization_barrier((value, *earlier))[0]


def near_far(a, move):
    return {0: a, 1: move(a, -1), 3: move(a, 1), 2: move(a, 2)}


def in_order(parts):
    return jnp.concatenate([parts[k] for k in range(4)], 0)


def spread(rows, z, y):
    count = rows.shape[0] // 4
    own = jnp.where(z == 3, rows[3 * count :], jnp.zeros_like(rows[:count]))
    for q in range(3):
        pairs = [(12 + k, q * 4 + k) for k in range(4)]
        own = own + lax.ppermute(rows[q * count : (q + 1) * count], "tower", pairs)
    return own


def collected(part, z, y):
    got = [lax.ppermute(part, "tower", [(q * 4 + k, 12 + k) for k in range(4)]) for q in range(3)]
    return jnp.concatenate(got + [jnp.where(z == 3, part, jnp.zeros_like(part))], 0)


def forward_tower(row_values, gain, projection):
    values = row_values.astype(f32)
    centred = values - jnp.mean(values, axis=1, keepdims=True)
    inverse = lax.rsqrt(jnp.mean(centred * centred, axis=1, keepdims=True) + epsilon_norm)
    normal_rows = centred * inverse
    normed = (normal_rows * gain).astype(bf)
    projected = jnp.dot(normed, projection, preferred_element_type=f32)
    length = jnp.sqrt(jnp.sum(projected * projected, axis=1, keepdims=True) + epsilon_unit)
    unit_exact = projected / length
    return (unit_exact.astype(bf), unit_exact, length, normal_rows, inverse)


pieces_rows = (96, 96, 96, 96, 192, 192, 192, 192, 192, 192)
starts = (0, 96, 192, 288, 384, 576, 768, 960, 1152, 1344)
place_one = {2: 0, 1: 2, 3: 3, 0: 6}
place_two = {2: 1, 1: 4, 3: 5, 0: 7}
params = pltpu.CompilerParams(vmem_limit_bytes=48 * 1024 * 1024)
whole = pl.BlockSpec(memory_space=pltpu.VMEM)
scalars = pl.BlockSpec(memory_space=pltpu.SMEM)
anywhere = pl.BlockSpec(memory_space=pl.ANY)
note_shape = jax.ShapeDtypeStruct((8, 128), f32)


def shaped(rows, width=1280, dtype=bf):
    return jax.ShapeDtypeStruct((rows, width), dtype)


def fetch(piece_refs, text, sems):
    copies = []
    for i, (ref, at, rows) in enumerate(zip(piece_refs, starts, pieces_rows)):
        copy = pltpu.make_async_copy(ref, text.at[pl.ds(at, rows)], sems.at[i])
        copy.start()
        copies.append(copy)
    for copy in copies:
        copy.wait()


def logits_kernel(scale, row_base, col_index, mine, other, *refs):
    piece_refs, (logits, row_out, col_out, text, high, summed, sems) = refs[:10], refs[10:]
    step = pl.program_id(0)

    @pl.when(step == 0)
    def _():
        fetch(piece_refs, text, sems)
        high[...] = jnp.full(high.shape, -3e38, f32)
        summed[...] = jnp.zeros(summed.shape, f32)
        row_out[...] = jnp.zeros(row_out.shape, f32)

    rows = jnp.concatenate([mine[...], other[...]], 0)
    tile = lax.dot_general(rows, text[...], (((1,), (1,)), ((), ())), preferred_element_type=f32)
    tile = tile * scale[0] + scale[1]
    logits[0] = tile[:128]
    logits[1] = tile[128:]
    row_high = jnp.max(tile, axis=1, keepdims=True)
    row_lse = row_high + jnp.log(jnp.sum(jnp.exp(tile - row_high), axis=1, keepdims=True))
    for h in range(2):
        across = jnp.transpose(jnp.broadcast_to(row_lse[h * 128 : h * 128 + 128], (128, 128)))
        row_out[pl.ds(4 * h + step, 1), :] = across[:1]
    latest = jnp.maximum(high[...], jnp.max(tile, axis=0, keepdims=True))
    summed[...] = summed[...] * jnp.exp(high[...] - latest) + jnp.sum(
        jnp.exp(tile - latest), axis=0, keepdims=True
    )
    high[...] = latest
    place = lax.broadcasted_iota(jnp.int32, (128, 1536), 0)
    matched = jnp.zeros((1, 1), f32)
    for h in range(2):
        hit = place + row_base[4 * h + step] == col_index[...]
        inside = jnp.where(hit, tile[h * 128 : h * 128 + 128], 0.0)
        matched += jnp.sum(jnp.sum(inside, axis=0, keepdims=True), axis=1, keepdims=True)
    row_out[8:16, :] += jnp.broadcast_to(matched, (8, 128))

    @pl.when(step == 3)
    def _():
        col_out[...] = high[...] + jnp.log(summed[...])


def make_logits(scale, row_base, col_index, mine, other, pieces):
    return pl.pallas_call(
        logits_kernel,
        grid=(4,),
        in_specs=[scalars, scalars, pl.BlockSpec((1, 1536), lambda i: (0, 0))]
        + [pl.BlockSpec((128, 1280), lambda i: (i, 0))] * 2
        + [anywhere] * 10,
        out_specs=[
            pl.BlockSpec((2, 128, 1536), lambda i: (0, i, 0)),
            pl.BlockSpec((16, 128), lambda i: (0, 0)),
            pl.BlockSpec((1, 1536), lambda i: (0, 0)),
        ],
        out_shape=[
            jax.ShapeDtypeStruct((2, 512, 1536), f32),
            jax.ShapeDtypeStruct((16, 128), f32),
            jax.ShapeDtypeStruct((1, 1536), f32),
        ],
        scratch_shapes=[
            pltpu.VMEM((1536, 1280), bf),
            pltpu.VMEM((1, 1536), f32),
            pltpu.VMEM((1, 1536), f32),
            pltpu.SemaphoreType.DMA((10,)),
        ],
        compiler_params=params,
        cost_estimate=pl.CostEstimate(flops=4026531840, bytes_accessed=13000000, transcendentals=3200000),
        name="logits",
    )(scale, row_base, col_index, mine, other, *pieces)


def ring_sum(values):
    return (values[0] + values[2]) + (values[1] + values[3])


def joined(parts):
    highest = parts[0]
    for part in parts[1:]:
        highest = jnp.maximum(highest, part)
    terms = [jnp.exp(part - highest) for part in parts]
    return highest + jnp.log(ring_sum(terms) if len(terms) == 4 else terms[0] + terms[1])


def col_kernel(by_block, last, own, got1, got2, got3, *outs):
    out = outs[0]
    got = {1: got1, 2: got2, 3: got3}
    sums = {}
    for half, place in enumerate((place_one, place_two)):
        for k in range(4):
            for j in range(4):
                row = 4 * place[k] + j
                parts = [own[row : row + 1, :]]
                for s in (1, 2, 3):
                    source = 4 * place[(k - s) % 4] + j if by_block[half] else 4 * place[k] + (j - s) % 4
                    parts.append(got[s][source : source + 1, :])
                value = joined(parts)
                out[row : row + 1, :] = value
                sums[half, k, j] = jnp.sum(value, axis=1, keepdims=True)
    if last:
        halves = [
            ring_sum([ring_sum([sums[half, k, j] for j in range(4)]) for k in range(4)])
            for half in range(2)
        ]
        outs[1][...] = jnp.broadcast_to(0.5 * (halves[0] + halves[1]), (8, 128))


def join_cols(own, move, by_block, last):
    got = [move(own, -s) for s in (1, 2, 3)]
    shapes = [jax.ShapeDtypeStruct((32, 48), f32)] + [note_shape] * last
    return pl.pallas_call(
        functools.partial(col_kernel, by_block, last),
        in_specs=[whole] * 4,
        out_specs=[whole] * len(shapes),
        out_shape=shapes,
        name="join_cols",
    )(own, *got)


def row_kernel(own, got1, got2, got3, out):
    got = {1: got1, 2: got2, 3: got3}
    for h in range(2):
        for k in range(4):
            row = 4 * h + k
            parts = [own[row : row + 1, :]]
            for s in (1, 2, 3):
                source = 4 * h + (k - s) % 4
                parts.append(got[s][source : source + 1, :])
            out[row : row + 1, :] = joined(parts)
    out[8:16, :] = ring_sum([own[8:16, :], got1[8:16, :], got2[8:16, :], got3[8:16, :]])


def join_rows(own):
    got = [moved_x(own, -s) for s in (1, 2, 3)]
    return pl.pallas_call(
        row_kernel,
        in_specs=[whole] * 4,
        out_specs=whole,
        out_shape=jax.ShapeDtypeStruct((16, 128), f32),
        name="join_rows",
    )(own, *got)


def pair_kernel(is_image, own, got, out, note):
    sums = {}
    for h in range(2):
        for k in range(4):
            row, source = 4 * h + k, 4 * (1 - h) + k
            value = joined([own[row : row + 1, :], got[source : source + 1, :]])
            out[row : row + 1, :] = value
            sums[h, k] = jnp.sum(value, axis=1, keepdims=True)
    of_rows = ring_sum([sums[0, k] for k in range(4)]) + ring_sum([sums[1, k] for k in range(4)])
    matched = own[8:16, :] + got[8:16, :]
    share = 0.5 * jnp.broadcast_to(of_rows, (8, 128)) - matched
    note[...] = jnp.where(is_image[0] > 0, share, 0.0)


def join_pair(is_image, own):
    got = swapped(own, "dp", 1)
    return pl.pallas_call(
        pair_kernel,
        in_specs=[scalars, whole, whole],
        out_specs=[whole, whole],
        out_shape=[jax.ShapeDtypeStruct((8, 128), f32), note_shape],
        name="join_pair",
    )(is_image, own, got)


def write_note(out, at, note):
    value = note[:1, :]
    high = value.astype(bf).astype(f32)
    middle = (value - high).astype(bf).astype(f32)
    low = value - high - middle
    lane = lax.broadcasted_iota(jnp.int32, (1, 128), 1)
    terms = jnp.where(lane == 0, high, jnp.where(lane == 1, middle, jnp.where(lane == 2, low, 0.0)))
    out[at : at + 16, :128] = jnp.broadcast_to(terms, (16, 128)).astype(bf)


def read_note(ref, at):
    terms = ref[at : at + 16, :128].astype(f32)[:1, :]
    lane = lax.broadcasted_iota(jnp.int32, (1, 128), 1)
    total = jnp.sum(jnp.where(lane < 3, terms, 0.0), axis=1, keepdims=True)
    return jnp.broadcast_to(total, (8, 128))


def grad_kernel(steps, rows_out, noted, scale, row_base, col_index, col_lse, row_lse, logits, mine, other, *refs):
    if noted:
        note, refs = refs[0], refs[1:]
    grad, outs, across = refs[0], refs[1:-1], refs[-1]
    step = pl.program_id(0)

    @pl.when(step == 0)
    def _():
        for r in range(8):
            across[r] = jnp.transpose(jnp.broadcast_to(row_lse[r : r + 1, :], (128, 128)))

    place = lax.broadcasted_iota(jnp.int32, (128, 384), 0)
    for r in range(8):
        h, k = r // 4, r % 4
        tile = logits[h, k * 128 : k * 128 + 128, :]
        of_row = jnp.concatenate([across[r]] * 3, 1)
        value = 0.5 * (jnp.exp(tile - of_row) + jnp.exp(tile - col_lse[...]))
        value = jnp.where(place + row_base[r] == col_index[...], value - 1.0, value)
        grad[h, k * 128 : k * 128 + 128, :] = value.astype(bf)
    dims = (((0,), (0,)), ((), ()))
    product = lax.dot_general(grad[0], mine[...], dims, preferred_element_type=f32)
    product += lax.dot_general(grad[1], other[...], dims, preferred_element_type=f32)
    product = (product * scale[0]).astype(bf)
    each = len(outs) // steps
    for s in range(steps):

        def store(s=s):
            for i in range(each):
                outs[s * each + i][:rows_out, :] = product[i * rows_out : i * rows_out + rows_out]

        if steps > 1:
            pl.when(step == s)(store)
        else:
            store()
    if noted:
        for out in outs[:2]:
            out[rows_out:, :] = jnp.zeros((16, 1280), bf)
            write_note(out, rows_out, note)


def make_grad(offset, steps, rows_out, scale, row_base, col_index, col_lse, row_lse, logits, mine, other, note=None):
    count = steps * 384 // rows_out
    outs = [shaped(rows_out + 16 if note is not None and i < 2 else rows_out) for i in range(count)]
    full = lambda s: pl.BlockSpec(s.shape, lambda i: (0,) * len(s.shape))
    extra = [] if note is None else [note]
    return pl.pallas_call(
        functools.partial(grad_kernel, steps, rows_out, note is not None),
        grid=(steps,),
        in_specs=[scalars, scalars]
        + [pl.BlockSpec((1, 384), lambda i: (0, offset + i))] * 2
        + [full(row_lse), pl.BlockSpec((2, 512, 384), lambda i: (0, 0, offset + i)), full(mine), full(other)]
        + [full(e) for e in extra],
        out_specs=[pl.BlockSpec((2, 512, 384), lambda i: (0, 0, i))] + [full(o) for o in outs],
        out_shape=[jax.ShapeDtypeStruct((2, 512, 384 * steps), bf)] + outs,
        scratch_shapes=[pltpu.VMEM((8, 128, 128), f32)],
        compiler_params=params,
        cost_estimate=pl.CostEstimate(flops=1006632960 * steps, bytes_accessed=6000000, transcendentals=786432 * steps),
        name="text_product",
    )(scale, row_base, col_index, col_lse, row_lse, logits, mine, other, *extra)


def near_kernel(note, one1, one3, two1, two3, one_left, one_right, two_left, two_right, *outs):
    a, b, c, d = outs
    add = lambda x, y: (x.astype(f32) + y.astype(f32)).astype(bf)
    a[:96] = add(one1[:96], one_left[:96])
    a[96:192] = one1[96:]
    a[192:208] = jnp.zeros((16, 1280), bf)
    write_note(a, 192, read_note(one_left, 96))
    b[:96] = one3[:96]
    b[96:192] = add(one3[96:], one_right[:96])
    c[:96] = add(two1[:96], two_left[...])
    c[96:192] = two1[96:]
    d[:96] = two3[:96]
    d[96:192] = add(two3[96:], two_right[...])


def near_sums(*args):
    outs = [shaped(208), shaped(192), shaped(192), shaped(192)]
    return pl.pallas_call(
        near_kernel, in_specs=[whole] * 9, out_specs=[whole] * 4, out_shape=outs, compiler_params=params, name="near_sums"
    )(*args)


def end_kernel(note, one_left_far, one_right_far, one0, two0, one_left, one_right, two_left, two_right, total_note, *outs):
    three = lambda a, b, c: (a.astype(f32) + b.astype(f32) + c.astype(f32)).astype(bf)
    value = ring_sum([note[...], read_note(one_right_far, 96), read_note(one_left, 192), read_note(one_left_far, 96)])
    total_note[...] = value
    for k in range(4):
        cut = slice(k * 48, k * 48 + 48)
        outs[k][:48, :] = three(one0[cut, :], one_left[cut, :], one_right[cut, :])
        if k:
            outs[k][48:, :] = jnp.zeros((16, 1280), bf)
            write_note(outs[k], 48, value)
        outs[4 + k][...] = three(two0[cut, :], two_left[cut, :], two_right[cut, :])


def end_sums(*args):
    outs = [note_shape, shaped(48), shaped(64), shaped(64), shaped(64)] + [shaped(48)] * 4
    return pl.pallas_call(
        end_kernel, in_specs=[whole] * 9, out_specs=[whole] * 9, out_shape=outs, compiler_params=params, name="end_sums"
    )(*args)


def image_kernel(first, scale, note, far, near, own, *refs):
    if not first:
        got, refs = refs[0], refs[1:]
    piece_refs, rest = refs[:10], refs[10:]
    outs, text, sems = rest[:-2], rest[-2], rest[-1]
    fetch(piece_refs, text, sems)
    if not first:
        value = note[...] + read_note(got, 512)
        outs[0][...] = value
    for k in range(4):
        cut = slice(k * 128, k * 128 + 128)
        product = jnp.dot(far[0, cut, :], text[:384], preferred_element_type=f32)
        product += jnp.dot(near[0, cut, :], text[384:1152], preferred_element_type=f32)
        product += jnp.dot(own[0, cut, :], text[1152:], preferred_element_type=f32)
        product = product * scale[0]
        if first:
            outs[0][cut, :] = product.astype(bf)
        else:
            outs[1 + k][:128, :] = (product + got[cut, :].astype(f32)).astype(bf)
            if k:
                outs[1 + k][128:, :] = jnp.zeros((16, 1280), bf)
                write_note(outs[1 + k], 128, value)
    if first:
        outs[0][512:, :] = jnp.zeros((16, 1280), bf)
        write_note(outs[0], 512, note)


def image_product(first, scale, note, far, near, own, pieces, got=None):
    outs = [shaped(528)] if first else [note_shape, shaped(128), shaped(144), shaped(144), shaped(144)]
    half = lambda a: pl.BlockSpec((1,) + a.shape[1:], lambda i: (1 if first else 0, 0, 0))
    full = lambda s: pl.BlockSpec(s.shape, lambda i: (0,) * len(s.shape))
    extra = [] if first else [got]
    return pl.pallas_call(
        functools.partial(image_kernel, first),
        grid=(1,),
        in_specs=[scalars, full(note), half(far), half(near), half(own)]
        + [full(e) for e in extra]
        + [anywhere] * 10,
        out_specs=[full(o) for o in outs],
        out_shape=outs,
        scratch_shapes=[pltpu.VMEM((1536, 1280), bf), pltpu.SemaphoreType.DMA((10,))],
        compiler_params=params,
        cost_estimate=pl.CostEstimate(flops=2013265920, bytes_accessed=7000000, transcendentals=0),
        name="image_product",
    )(scale, note, far, near, own, *extra, *pieces)


def backward_rows(grad_unit, unit_exact, length, normal_rows, inverse, gain, projection):
    dot_along = jnp.sum(unit_exact * grad_unit, axis=1, keepdims=True)
    grad_projected = ((grad_unit - unit_exact * dot_along) / length).astype(bf)
    grad_normed = lax.dot_general(
        grad_projected, projection, (((1,), (1,)), ((), ())), preferred_element_type=f32
    )
    scaled = grad_normed * gain
    centre = jnp.mean(scaled, axis=1, keepdims=True)
    tilt_mean = jnp.mean(scaled * normal_rows, axis=1, keepdims=True)
    return inverse * (scaled - centre - normal_rows * tilt_mean)


def image_back_kernel(is_image, note, own, left, right, far, unit, length, normal, inverse, gain, projection, out, total):
    total[...] = ring_sum([note[...], read_note(right, 128), read_note(far, 128), read_note(left, 128)])
    rows = lambda ref: ref[:128, :].astype(f32)
    grad_unit = (rows(own) + rows(far)) + (rows(left) + rows(right))
    value = backward_rows(
        grad_unit, unit[...], length[...], normal[...], inverse[...], gain[...], projection[...]
    )
    out[...] = jnp.where(is_image[0] > 0, value, 0.0).astype(bf)


def image_backward(*args):
    return pl.pallas_call(
        image_back_kernel,
        in_specs=[scalars] + [whole] * 11,
        out_specs=[whole] * 2,
        out_shape=[shaped(128, 1664), note_shape],
        compiler_params=params,
        name="image_backward",
    )(*args)


def text_back_kernel(tower, lane, a0, a1, a3, a2, b0, b1, b3, b2, unit, length, normal, inverse, gain, projection, out, total):
    of_tower = ring_sum([tower[...], read_note(a3, 48), read_note(a2, 48), read_note(a1, 48)])
    total[...] = of_tower + lane[...]
    rows = lambda ref: ref[:48, :].astype(f32)
    one = (rows(a0) + rows(a2)) + (rows(a1) + rows(a3))
    two = (rows(b0) + rows(b2)) + (rows(b1) + rows(b3))
    value = backward_rows(
        jnp.concatenate([one, two], 0),
        unit[...], length[...], normal[...], inverse[...], gain[...], projection[...],
    )
    out[...] = value.astype(bf)


def text_backward(*args):
    return pl.pallas_call(
        text_back_kernel,
        in_specs=[whole] * 16,
        out_specs=[whole] * 2,
        out_shape=[shaped(96), note_shape],
        compiler_params=params,
        name="text_backward",
    )(*args)


def column_tables():
    of_y, of_z, inside = [], [], []
    for place, half in ((2, 0), (2, 1), (1, 0), (3, 0), (1, 1), (3, 1), (0, 0), (0, 1)):
        for j in range(4):
            for r in range(48):
                of_y.append(j if half else place)
                of_z.append(place if half else j)
                inside.append(48 * half + r)
    return [np.array(a, np.int32)[None, :] for a in (of_y, of_z, inside)]


def local(
    image_hidden, text_hidden, image_gain, text_gain, image_projection, text_projection, logit_scale
):
    tower_at = lax.axis_index("tower")
    lane_at = lax.axis_index("dp")
    z, y, x, c = tower_at // 4, tower_at % 4, lane_at // 2, lane_at % 2
    is_image = z < 3
    flag = jnp.reshape(is_image.astype(jnp.int32), (1,))
    image_rows = image_hidden[0, 0]
    text_rows = spread(text_hidden[0, 0], z, y)
    scale = jnp.concatenate([logit_scale, jnp.reshape(jnp.where(is_image, 0.0, lowest), (1,))])
    of_y, of_z, inside = column_tables()
    col_index = lane_at * 1536 + (y + of_y) % 4 * 384 + (z + of_z) % 4 * 96 + inside
    steps = np.array([0, 1, 2, 3] * 2, np.int32)
    core = np.array([0] * 4 + [1] * 4, np.int32)
    row_base = tower_at * 1024 + (2 * ((x + steps) % 4) + (c + core) % 2) * 128
    row_base = jnp.where(is_image, row_base, -(1 << 20))

    image_parts = forward_tower(image_rows, image_gain, image_projection)
    image_unit = jnp.where(is_image, image_parts[0], jnp.zeros_like(image_parts[0]))
    image_near = near_far(image_unit, moved_x)
    text_rows = after(text_rows, image_unit)
    text_parts = forward_tower(text_rows, text_gain, text_projection)
    text_unit = text_parts[0]
    one_own = in_order(near_far(text_unit[:48], moved_z))
    two_own = in_order(near_far(text_unit[48:], moved_y))
    one_left, one_right = moved_y(one_own, 1), moved_y(one_own, -1)
    two_left, two_right = moved_z(two_own, 1), moved_z(two_own, -1)
    mine = in_order(after(image_near, one_own, two_own))
    other = swapped(mine, "dp", 1)
    pieces = [
        moved_y(one_left[:96], 1), moved_y(one_right[96:], -1),
        moved_z(two_left[:96], 1), moved_z(two_right[96:], -1),
        one_right, one_left, two_right, two_left, one_own, two_own,
    ]

    logits, row_part, col_part = make_logits(scale, row_base, col_index, mine, other, pieces)
    col_stat = join_cols(col_part.reshape(32, 48), moved_z, (False, True), False)[0]
    row_stat = join_rows(row_part)
    col_stat, of_lane = join_cols(col_stat, moved_y, (True, False), True)
    row_lse, of_tower = join_pair(flag, row_stat)
    col_lse = col_stat.reshape(1, 1536)

    common = (scale, row_base, col_index, col_lse, row_lse, logits, mine, other)
    far, one_a, one_b, two_a, two_b = make_grad(0, 1, 96, *common, note=of_tower)
    one_far_left, one_far_right = moved_y(one_a, 1), moved_y(one_b, -1)
    two_far_left, two_far_right = moved_z(two_a, 1), moved_z(two_b, -1)
    near, one1, one3, two1, two3 = make_grad(1, 2, 192, *common)
    one_far_left, near = lax.optimization_barrier((one_far_left, near))
    to_right, to_left, two_to_right, two_to_left = near_sums(
        of_tower, one1, one3, two1, two3, one_far_left, one_far_right, two_far_left, two_far_right
    )
    one_left, one_right = moved_y(to_right, 1), moved_y(to_left, -1)
    two_left, two_right = moved_z(two_to_right, 1), moved_z(two_to_left, -1)
    row_lse = after(row_lse, to_right)
    common = (scale, row_base, col_index, col_lse, row_lse, logits, mine, other)
    own, one0, two0 = make_grad(3, 1, 192, *common)
    other_part = image_product(True, scale, of_lane, far, near, own, pieces)[0]
    got = swapped(other_part, "dp", 1)
    of_lane, image_own, to1, to2, to3 = image_product(
        False, scale, of_lane, far, near, own, pieces, got
    )
    image_in = [image_own, moved_x(to1, 1), moved_x(to3, 3), moved_x(to2, 2)]
    one_left = after(one_left, image_own)
    of_tower, *ends = end_sums(
        of_tower, one_far_left, one_far_right, one0, two0, one_left, one_right, two_left, two_right
    )
    one_in = [ends[0], moved_z(ends[1], 1), moved_z(ends[3], -1), moved_z(ends[2], 2)]
    two_in = [ends[4], moved_y(ends[5], 1), moved_y(ends[7], -1), moved_y(ends[6], 2)]
    image_own = after(image_own, ends[0])
    image_out, of_lane = image_backward(
        flag, of_lane, image_own, *image_in[1:], *image_parts[1:], image_gain[None, :], image_projection
    )
    one_own_sum = after(one_in[0], image_out)
    text_out, loss = text_backward(
        of_tower, of_lane, one_own_sum, *one_in[1:], *two_in, *text_parts[1:], text_gain[None, :], text_projection
    )
    text_out = collected(text_out, z, y)
    return (image_out[None, None], text_out[None, None], loss[0, :1] / 12288)


def solution(mesh):
    in_specs = (P("tower", "dp", None, None), P("tower", "dp", None, None), P(), P(), P(), P(), P())
    out_specs = (P("tower", "dp", None, None), P("tower", "dp", None, None), P())
    return jax.shard_map(local, mesh=mesh, in_specs=in_specs, out_specs=out_specs, check_vma=False)
```

```python
import functools

import jax
import jax.numpy as jnp
import numpy as np
from jax import lax
from jax.experimental import pallas as pl
from jax.experimental.pallas import tpu as pltpu
from jax.sharding import PartitionSpec as P

bf = jnp.bfloat16
f32 = jnp.float32
epsilon_norm = 1e-05
epsilon_unit = 1e-06
lowest = -1e30


def moved_z(a, step):
    pairs = [(z * 4 + y, (z + step) % 4 * 4 + y) for z in range(4) for y in range(4)]
    return lax.ppermute(a, "tower", pairs)


def moved_y(a, step):
    pairs = [(z * 4 + y, z * 4 + (y + step) % 4) for z in range(4) for y in range(4)]
    return lax.ppermute(a, "tower", pairs)


def moved_x(a, step):
    pairs = [(x * 2 + c, (x + step) % 4 * 2 + c) for x in range(4) for c in range(2)]
    return lax.ppermute(a, "dp", pairs)


def swapped(a, axis, bit):
    count = lax.axis_size(axis)
    return lax.ppermute(a, axis, [(i, i ^ bit) for i in range(count)])


def after(value, *earlier):
    return lax.optimization_barrier((value, *earlier))[0]


def near_far(a, move):
    return {0: a, 1: move(a, -1), 3: move(a, 1), 2: move(a, 2)}


def in_order(parts):
    return jnp.concatenate([parts[k] for k in range(4)], 0)


def spread(rows, z, y):
    count = rows.shape[0] // 4
    own = jnp.where(z == 3, rows[3 * count :], jnp.zeros_like(rows[:count]))
    for q in range(3):
        pairs = [(12 + k, q * 4 + k) for k in range(4)]
        own = own + lax.ppermute(rows[q * count : (q + 1) * count], "tower", pairs)
    return own


def collected(part, z, y):
    got = [lax.ppermute(part, "tower", [(q * 4 + k, 12 + k) for k in range(4)]) for q in range(3)]
    return jnp.concatenate(got + [jnp.where(z == 3, part, jnp.zeros_like(part))], 0)


pieces = 16
piece_rows = 96
small_cost = pl.CostEstimate(flops=1000, bytes_accessed=1000, transcendentals=0)
place_one = {2: 0, 1: 2, 3: 3, 0: 6}
place_two = {2: 1, 1: 4, 3: 5, 0: 7}
params = pltpu.CompilerParams(vmem_limit_bytes=48 * 1024 * 1024)
whole = pl.BlockSpec(memory_space=pltpu.VMEM)
scalars = pl.BlockSpec(memory_space=pltpu.SMEM)
anywhere = pl.BlockSpec(memory_space=pl.ANY)
note_shape = jax.ShapeDtypeStruct((8, 128), f32)


def shaped(rows, width=1280, dtype=bf):
    return jax.ShapeDtypeStruct((rows, width), dtype)


def fetch(piece_refs, text, sems):
    copies = []
    for i, ref in enumerate(piece_refs):
        copy = pltpu.make_async_copy(ref, text.at[pl.ds(i * piece_rows, piece_rows)], sems.at[i])
        copy.start()
        copies.append(copy)
    for copy in copies:
        copy.wait()


def logits_kernel(scale, row_base, col_index, mine, other, *refs):
    piece_refs, (logits, row_out, col_out, text, high, summed, sems) = refs[:pieces], refs[pieces:]
    step = pl.program_id(0)

    @pl.when(step == 0)
    def _():
        fetch(piece_refs, text, sems)
        high[...] = jnp.full(high.shape, -3e38, f32)
        summed[...] = jnp.zeros(summed.shape, f32)
        row_out[...] = jnp.zeros(row_out.shape, f32)

    rows = jnp.concatenate([mine[...], other[...]], 0)
    tile = lax.dot_general(rows, text[...], (((1,), (1,)), ((), ())), preferred_element_type=f32)
    tile = tile * scale[0] + scale[1]
    logits[0] = tile[:128]
    logits[1] = tile[128:]
    row_high = jnp.max(tile, axis=1, keepdims=True)
    row_lse = row_high + jnp.log(jnp.sum(jnp.exp(tile - row_high), axis=1, keepdims=True))
    for h in range(2):
        across = jnp.transpose(jnp.broadcast_to(row_lse[h * 128 : h * 128 + 128], (128, 128)))
        row_out[pl.ds(4 * h + step, 1), :] = across[:1]
    latest = jnp.maximum(high[...], jnp.max(tile, axis=0, keepdims=True))
    summed[...] = summed[...] * jnp.exp(high[...] - latest) + jnp.sum(
        jnp.exp(tile - latest), axis=0, keepdims=True
    )
    high[...] = latest
    place = lax.broadcasted_iota(jnp.int32, (128, 1536), 0)
    matched = jnp.zeros((1, 1), f32)
    for h in range(2):
        hit = place + row_base[4 * h + step] == col_index[...]
        inside = jnp.where(hit, tile[h * 128 : h * 128 + 128], 0.0)
        matched += jnp.sum(jnp.sum(inside, axis=0, keepdims=True), axis=1, keepdims=True)
    row_out[8:16, :] += jnp.broadcast_to(matched, (8, 128))

    @pl.when(step == 3)
    def _():
        value = high[...] + jnp.log(summed[...])
        for i in range(32):
            col_out[i : i + 1, :] = value[:, 48 * i : 48 * i + 48]


def make_logits(scale, row_base, col_index, mine, other, text_pieces):
    return pl.pallas_call(
        logits_kernel,
        grid=(4,),
        in_specs=[scalars, scalars, pl.BlockSpec((1, 1536), lambda i: (0, 0))]
        + [pl.BlockSpec((128, 1280), lambda i: (i, 0))] * 2
        + [anywhere] * pieces,
        out_specs=[
            pl.BlockSpec((2, 128, 1536), lambda i: (0, i, 0)),
            pl.BlockSpec((16, 128), lambda i: (0, 0)),
            pl.BlockSpec((32, 48), lambda i: (0, 0)),
        ],
        out_shape=[
            jax.ShapeDtypeStruct((2, 512, 1536), f32),
            jax.ShapeDtypeStruct((16, 128), f32),
            jax.ShapeDtypeStruct((32, 48), f32),
        ],
        scratch_shapes=[
            pltpu.VMEM((1536, 1280), bf),
            pltpu.VMEM((1, 1536), f32),
            pltpu.VMEM((1, 1536), f32),
            pltpu.SemaphoreType.DMA((pieces,)),
        ],
        compiler_params=params,
        cost_estimate=small_cost,
        name="logits",
    )(scale, row_base, col_index, mine, other, *text_pieces)


def ring_sum(values):
    return (values[0] + values[2]) + (values[1] + values[3])


def joined(parts):
    highest = parts[0]
    for part in parts[1:]:
        highest = jnp.maximum(highest, part)
    terms = [jnp.exp(part - highest) for part in parts]
    return highest + jnp.log(ring_sum(terms) if len(terms) == 4 else terms[0] + terms[1])


def join_cols(by_block, own, got):
    rows, sums = {}, {}
    for half, place in enumerate((place_one, place_two)):
        for k in range(4):
            for j in range(4):
                row = 4 * place[k] + j
                parts = [own[row : row + 1, :]]
                for s in (1, 2, 3):
                    source = 4 * place[(k - s) % 4] + j if by_block[half] else 4 * place[k] + (j - s) % 4
                    parts.append(got[s - 1][source : source + 1, :])
                rows[row] = joined(parts)
                sums[half, k, j] = rows[row]
    return rows, sums


def first_kernel(col, col1, col2, col3, row, row1, row2, row3, col_out, row_out):
    rows, _ = join_cols((False, True), col, (col1, col2, col3))
    for i, value in rows.items():
        col_out[i : i + 1, :] = value
    got = (row1, row2, row3)
    for h in range(2):
        for k in range(4):
            at = 4 * h + k
            parts = [row[at : at + 1, :]]
            for s in (1, 2, 3):
                source = 4 * h + (k - s) % 4
                parts.append(got[s - 1][source : source + 1, :])
            row_out[at : at + 1, :] = joined(parts)
    row_out[8:16, :] = ring_sum([row[8:16, :], row1[8:16, :], row2[8:16, :], row3[8:16, :]])


def second_kernel(is_image, col, col1, col2, col3, row, row_got, col_out, row_out, of_lane, of_tower):
    rows, sums = join_cols((True, False), col, (col1, col2, col3))
    for i, value in rows.items():
        col_out[:, 48 * i : 48 * i + 48] = value
    halves = [
        ring_sum([ring_sum([sums[half, k, j] for j in range(4)]) for k in range(4)]) for half in range(2)
    ]
    of_cols = jnp.sum(halves[0] + halves[1], axis=1, keepdims=True)
    of_lane[...] = jnp.broadcast_to(0.5 * of_cols, (8, 128))
    values = {}
    for h in range(2):
        for k in range(4):
            at, source = 4 * h + k, 4 * (1 - h) + k
            value = joined([row[at : at + 1, :], row_got[source : source + 1, :]])
            row_out[at : at + 1, :] = value
            values[h, k] = value
    pair = [ring_sum([values[h, k] for k in range(4)]) for h in range(2)]
    of_rows = jnp.sum(pair[0] + pair[1], axis=1, keepdims=True)
    matched = row[8:16, :] + row_got[8:16, :]
    share = 0.5 * jnp.broadcast_to(of_rows, (8, 128)) - matched
    of_tower[...] = jnp.where(is_image[0] > 0, share, 0.0)


def statistics(is_image, col, row):
    full = lambda s: pl.BlockSpec(s.shape, lambda i: (0,) * len(s.shape))
    col_got = [moved_z(col, -s) for s in (1, 2, 3)]
    row_got = [moved_x(row, -s) for s in (1, 2, 3)]
    shapes = [jax.ShapeDtypeStruct((32, 48), f32), jax.ShapeDtypeStruct((16, 128), f32)]
    col, row = pl.pallas_call(
        first_kernel,
        grid=(1,),
        in_specs=[full(col)] * 4 + [full(row)] * 4,
        out_specs=[full(s) for s in shapes],
        out_shape=shapes,
        cost_estimate=small_cost,
        name="first_merge",
    )(col, *col_got, row, *row_got)
    col_got = [moved_y(col, -s) for s in (1, 2, 3)]
    shapes = [jax.ShapeDtypeStruct((1, 1536), f32), jax.ShapeDtypeStruct((8, 128), f32), note_shape, note_shape]
    return pl.pallas_call(
        second_kernel,
        grid=(1,),
        in_specs=[scalars] + [full(col)] * 4 + [full(row)] * 2,
        out_specs=[full(s) for s in shapes],
        out_shape=shapes,
        cost_estimate=small_cost,
        name="second_merge",
    )(is_image, col, *col_got, row, swapped(row, "dp", 1))


def write_note(out, at, note):
    value = note[:1, :]
    high = value.astype(bf).astype(f32)
    middle = (value - high).astype(bf).astype(f32)
    low = value - high - middle
    lane = lax.broadcasted_iota(jnp.int32, (1, 128), 1)
    terms = jnp.where(lane == 0, high, jnp.where(lane == 1, middle, jnp.where(lane == 2, low, 0.0)))
    out[at : at + 16, :128] = jnp.broadcast_to(terms, (16, 128)).astype(bf)


def read_note(ref, at):
    terms = ref[at : at + 16, :128].astype(f32)[:1, :]
    lane = lax.broadcasted_iota(jnp.int32, (1, 128), 1)
    total = jnp.sum(jnp.where(lane < 3, terms, 0.0), axis=1, keepdims=True)
    return jnp.broadcast_to(total, (8, 128))


def grad_kernel(steps, rows_out, noted, scale, row_base, col_index, col_lse, row_lse, logits, mine, other, *refs):
    if noted:
        note, refs = refs[0], refs[1:]
    grad, outs, across = refs[0], refs[1:-1], refs[-1]
    step = pl.program_id(0)

    @pl.when(step == 0)
    def _():
        for r in range(8):
            across[r] = jnp.transpose(jnp.broadcast_to(row_lse[r : r + 1, :], (128, 128)))

    place = lax.broadcasted_iota(jnp.int32, (128, 384), 0)
    for r in range(8):
        h, k = r // 4, r % 4
        tile = logits[h, k * 128 : k * 128 + 128, :]
        of_row = jnp.concatenate([across[r]] * 3, 1)
        value = 0.5 * (jnp.exp(tile - of_row) + jnp.exp(tile - col_lse[...]))
        value = jnp.where(place + row_base[r] == col_index[...], value - 1.0, value)
        grad[h, k * 128 : k * 128 + 128, :] = value.astype(bf)
    dims = (((0,), (0,)), ((), ()))
    product = lax.dot_general(grad[0], mine[...], dims, preferred_element_type=f32)
    product += lax.dot_general(grad[1], other[...], dims, preferred_element_type=f32)
    product = (product * scale[0]).astype(bf)
    each = len(outs) // steps
    for s in range(steps):

        def store(s=s):
            for i in range(each):
                outs[s * each + i][:rows_out, :] = product[i * rows_out : i * rows_out + rows_out]

        if steps > 1:
            pl.when(step == s)(store)
        else:
            store()
    if noted:
        for out in outs[:2]:
            out[rows_out:, :] = jnp.zeros((16, 1280), bf)
            write_note(out, rows_out, note)


def make_grad(offset, steps, rows_out, scale, row_base, col_index, col_lse, row_lse, logits, mine, other, note=None):
    count = steps * 384 // rows_out
    outs = [shaped(rows_out + 16 if note is not None and i < 2 else rows_out) for i in range(count)]
    full = lambda s: pl.BlockSpec(s.shape, lambda i: (0,) * len(s.shape))
    extra = [] if note is None else [note]
    return pl.pallas_call(
        functools.partial(grad_kernel, steps, rows_out, note is not None),
        grid=(steps,),
        in_specs=[scalars, scalars]
        + [pl.BlockSpec((1, 384), lambda i: (0, offset + i))] * 2
        + [full(row_lse), pl.BlockSpec((2, 512, 384), lambda i: (0, 0, offset + i)), full(mine), full(other)]
        + [full(e) for e in extra],
        out_specs=[pl.BlockSpec((2, 512, 384), lambda i: (0, 0, i))] + [full(o) for o in outs],
        out_shape=[jax.ShapeDtypeStruct((2, 512, 384 * steps), bf)] + outs,
        scratch_shapes=[pltpu.VMEM((8, 128, 128), f32)],
        compiler_params=params,
        cost_estimate=small_cost,
        name="text_product",
    )(scale, row_base, col_index, col_lse, row_lse, logits, mine, other, *extra)


def near_kernel(note, one1, one3, two1, two3, one_left, one_right, two_left, two_right, *outs):
    a, b, c, d = outs
    add = lambda x, y: (x.astype(f32) + y.astype(f32)).astype(bf)
    a[:96] = add(one1[:96], one_left[:96])
    a[96:192] = one1[96:]
    a[192:208] = jnp.zeros((16, 1280), bf)
    write_note(a, 192, read_note(one_left, 96))
    b[:96] = one3[:96]
    b[96:192] = add(one3[96:], one_right[:96])
    c[:96] = add(two1[:96], two_left[...])
    c[96:192] = two1[96:]
    d[:96] = two3[:96]
    d[96:192] = add(two3[96:], two_right[...])


def near_sums(*args):
    outs = [shaped(208), shaped(192), shaped(192), shaped(192)]
    return pl.pallas_call(
        near_kernel, in_specs=[whole] * 9, out_specs=[whole] * 4, out_shape=outs, compiler_params=params, cost_estimate=small_cost, name="near_sums"
    )(*args)


def end_kernel(note, one_left_far, one_right_far, one0, two0, one_left, one_right, two_left, two_right, total_note, *outs):
    three = lambda a, b, c: (a.astype(f32) + b.astype(f32) + c.astype(f32)).astype(bf)
    value = ring_sum([note[...], read_note(one_right_far, 96), read_note(one_left, 192), read_note(one_left_far, 96)])
    total_note[...] = value
    for k in range(4):
        cut = slice(k * 48, k * 48 + 48)
        outs[k][:48, :] = three(one0[cut, :], one_left[cut, :], one_right[cut, :])
        if k:
            outs[k][48:, :] = jnp.zeros((16, 1280), bf)
            write_note(outs[k], 48, value)
        outs[4 + k][...] = three(two0[cut, :], two_left[cut, :], two_right[cut, :])


def end_sums(*args):
    outs = [note_shape, shaped(48), shaped(64), shaped(64), shaped(64)] + [shaped(48)] * 4
    return pl.pallas_call(
        end_kernel, in_specs=[whole] * 9, out_specs=[whole] * 9, out_shape=outs, compiler_params=params, cost_estimate=small_cost, name="end_sums"
    )(*args)


def image_kernel(first, scale, note, far, near, own, *refs):
    if not first:
        got, refs = refs[0], refs[1:]
    piece_refs, rest = refs[:pieces], refs[pieces:]
    outs, text, sems = rest[:-2], rest[-2], rest[-1]
    fetch(piece_refs, text, sems)
    if not first:
        value = note[...] + read_note(got, 512)
        outs[0][...] = value
    for k in range(4):
        cut = slice(k * 128, k * 128 + 128)
        product = jnp.dot(far[0, cut, :], text[:384], preferred_element_type=f32)
        product += jnp.dot(near[0, cut, :], text[384:1152], preferred_element_type=f32)
        product += jnp.dot(own[0, cut, :], text[1152:], preferred_element_type=f32)
        product = product * scale[0]
        if first:
            outs[0][cut, :] = product.astype(bf)
        else:
            outs[1 + k][:128, :] = (product + got[cut, :].astype(f32)).astype(bf)
            if k:
                outs[1 + k][128:, :] = jnp.zeros((16, 1280), bf)
                write_note(outs[1 + k], 128, value)
    if first:
        outs[0][512:, :] = jnp.zeros((16, 1280), bf)
        write_note(outs[0], 512, note)


def image_product(first, scale, note, far, near, own, text_pieces, got=None):
    outs = [shaped(528)] if first else [note_shape, shaped(128), shaped(144), shaped(144), shaped(144)]
    half = lambda a: pl.BlockSpec((1,) + a.shape[1:], lambda i: (1 if first else 0, 0, 0))
    full = lambda s: pl.BlockSpec(s.shape, lambda i: (0,) * len(s.shape))
    extra = [] if first else [got]
    return pl.pallas_call(
        functools.partial(image_kernel, first),
        grid=(1,),
        in_specs=[scalars, full(note), half(far), half(near), half(own)]
        + [full(e) for e in extra]
        + [anywhere] * pieces,
        out_specs=[full(o) for o in outs],
        out_shape=outs,
        scratch_shapes=[pltpu.VMEM((1536, 1280), bf), pltpu.SemaphoreType.DMA((pieces,))],
        compiler_params=params,
        cost_estimate=small_cost,
        name="image_product",
    )(scale, note, far, near, own, *extra, *text_pieces)


def backward_rows(grad_unit, unit_exact, length, normal_rows, inverse, gain, projection):
    dot_along = jnp.sum(unit_exact * grad_unit, axis=1, keepdims=True)
    grad_projected = ((grad_unit - unit_exact * dot_along) / length).astype(bf)
    grad_normed = lax.dot_general(
        grad_projected, projection, (((1,), (1,)), ((), ())), preferred_element_type=f32
    )
    scaled = grad_normed * gain
    centre = jnp.mean(scaled, axis=1, keepdims=True)
    tilt_mean = jnp.mean(scaled * normal_rows, axis=1, keepdims=True)
    return inverse * (scaled - centre - normal_rows * tilt_mean)


def image_back_kernel(is_image, note, own, left, right, far, unit, length, normal, inverse, gain, projection, out, total):
    total[...] = ring_sum([note[...], read_note(right, 128), read_note(far, 128), read_note(left, 128)])
    rows = lambda ref: ref[:128, :].astype(f32)
    grad_unit = (rows(own) + rows(far)) + (rows(left) + rows(right))
    value = backward_rows(
        grad_unit, unit[...], length[...], normal[...], inverse[...], gain[...], projection[...]
    )
    out[...] = jnp.where(is_image[0] > 0, value, 0.0).astype(bf)


def image_backward(*args):
    return pl.pallas_call(
        image_back_kernel,
        in_specs=[scalars] + [whole] * 11,
        out_specs=[whole] * 2,
        out_shape=[shaped(128, 1664), note_shape],
        compiler_params=params,
        cost_estimate=small_cost,
        name="image_backward",
    )(*args)


def text_back_kernel(tower, lane, a0, a1, a3, a2, b0, b1, b3, b2, unit, length, normal, inverse, gain, projection, out, total):
    of_tower = ring_sum([tower[...], read_note(a3, 48), read_note(a2, 48), read_note(a1, 48)])
    total[...] = of_tower + lane[...]
    rows = lambda ref: ref[:48, :].astype(f32)
    one = (rows(a0) + rows(a2)) + (rows(a1) + rows(a3))
    two = (rows(b0) + rows(b2)) + (rows(b1) + rows(b3))
    value = backward_rows(
        jnp.concatenate([one, two], 0),
        unit[...], length[...], normal[...], inverse[...], gain[...], projection[...],
    )
    out[...] = value.astype(bf)


def text_backward(*args):
    return pl.pallas_call(
        text_back_kernel,
        in_specs=[whole] * 16,
        out_specs=[whole] * 2,
        out_shape=[shaped(96), note_shape],
        compiler_params=params,
        cost_estimate=small_cost,
        name="text_backward",
    )(*args)


def forward_kernel(cuts, keep, rows, gain, projection, *outs):
    values = rows[...].astype(f32)
    centred = values - jnp.mean(values, axis=1, keepdims=True)
    inverse = lax.rsqrt(jnp.mean(centred * centred, axis=1, keepdims=True) + epsilon_norm)
    normal = centred * inverse
    normed = (normal * gain[...]).astype(bf)
    projected = jnp.dot(normed, projection[...], preferred_element_type=f32)
    length = jnp.sqrt(jnp.sum(projected * projected, axis=1, keepdims=True) + epsilon_unit)
    unit = projected / length
    rounded = jnp.where(keep[0] > 0, unit, 0.0).astype(bf)
    each = rounded.shape[0] // cuts
    for i in range(cuts):
        outs[i][...] = rounded[i * each : i * each + each]
    unit_out, length_out, normal_out, inverse_out = outs[cuts:]
    unit_out[...] = unit
    length_out[...] = length
    normal_out[...] = normal
    inverse_out[...] = inverse


def forward_tower(cuts, keep, rows, gain, projection):
    count, width = rows.shape
    outs = [shaped(count // cuts)] * cuts + [
        shaped(count, 1280, f32), shaped(count, 1, f32), shaped(count, width, f32), shaped(count, 1, f32)
    ]
    return pl.pallas_call(
        functools.partial(forward_kernel, cuts),
        in_specs=[scalars] + [whole] * 3,
        out_specs=[whole] * len(outs),
        out_shape=outs,
        compiler_params=params,
        cost_estimate=small_cost,
        name="forward",
    )(keep, rows, gain, projection)


def column_tables():
    of_y, of_z, inside = [], [], []
    for place, half in ((2, 0), (2, 1), (1, 0), (3, 0), (1, 1), (3, 1), (0, 0), (0, 1)):
        for j in range(4):
            for r in range(48):
                of_y.append(j if half else place)
                of_z.append(place if half else j)
                inside.append(48 * half + r)
    return [np.array(a, np.int32)[None, :] for a in (of_y, of_z, inside)]


def local(
    image_hidden, text_hidden, image_gain, text_gain, image_projection, text_projection, logit_scale
):
    tower_at = lax.axis_index("tower")
    lane_at = lax.axis_index("dp")
    z, y, x, c = tower_at // 4, tower_at % 4, lane_at // 2, lane_at % 2
    is_image = z < 3
    flag = jnp.reshape(is_image.astype(jnp.int32), (1,))
    image_rows = image_hidden[0, 0]
    text_rows = spread(text_hidden[0, 0], z, y)
    scale = jnp.concatenate([logit_scale, jnp.reshape(jnp.where(is_image, 0.0, lowest), (1,))])
    of_y, of_z, inside = column_tables()
    col_index = lane_at * 1536 + (y + of_y) % 4 * 384 + (z + of_z) % 4 * 96 + inside
    steps = np.array([0, 1, 2, 3] * 2, np.int32)
    core = np.array([0] * 4 + [1] * 4, np.int32)
    row_base = tower_at * 1024 + (2 * ((x + steps) % 4) + (c + core) % 2) * 128
    row_base = jnp.where(is_image, row_base, -(1 << 20))

    every = jnp.ones((1,), jnp.int32)
    image_gain, text_gain = image_gain[None, :], text_gain[None, :]
    image_parts = forward_tower(1, flag, image_rows, image_gain, image_projection)
    image_near = near_far(image_parts[0], moved_x)
    text_rows = after(text_rows, image_parts[0])
    one_unit, two_unit, *text_parts = forward_tower(2, every, text_rows, text_gain, text_projection)
    one, two = near_far(one_unit, moved_z), near_far(two_unit, moved_y)
    one_low = jnp.concatenate([one[0], one[1]], 0)
    two_low = jnp.concatenate([two[0], two[1]], 0)
    one_high = jnp.concatenate([one[2], one[3]], 0)
    two_high = jnp.concatenate([two[2], two[3]], 0)
    one_left, two_left = moved_y(one_low, 1), moved_z(two_low, 1)
    one_right, two_right = moved_y(one_high, -1), moved_z(two_high, -1)
    mine = in_order(after(image_near, one_high, two_high))
    other = swapped(mine, "dp", 1)
    text_pieces = [
        moved_y(one_left, 1), moved_y(one_right, -1), moved_z(two_left, 1), moved_z(two_right, -1),
        moved_y(one_low, -1), one_right, one_left, moved_y(one_high, 1),
        moved_z(two_low, -1), two_right, two_left, moved_z(two_high, 1),
        one_low, one_high, two_low, two_high,
    ]

    logits, row_part, col_part = make_logits(scale, row_base, col_index, mine, other, text_pieces)
    col_lse, row_lse, of_lane, of_tower = statistics(flag, col_part, row_part)

    common = (scale, row_base, col_index, col_lse, row_lse, logits, mine, other)
    far, one_a, one_b, two_a, two_b = make_grad(0, 1, 96, *common, note=of_tower)
    one_far_left, one_far_right = moved_y(one_a, 1), moved_y(one_b, -1)
    two_far_left, two_far_right = moved_z(two_a, 1), moved_z(two_b, -1)
    near, one1, one3, two1, two3 = make_grad(1, 2, 192, *common)
    one_far_left, near = lax.optimization_barrier((one_far_left, near))
    to_right, to_left, two_to_right, two_to_left = near_sums(
        of_tower, one1, one3, two1, two3, one_far_left, one_far_right, two_far_left, two_far_right
    )
    one_left, one_right = moved_y(to_right, 1), moved_y(to_left, -1)
    two_left, two_right = moved_z(two_to_right, 1), moved_z(two_to_left, -1)
    row_lse = after(row_lse, to_right)
    common = (scale, row_base, col_index, col_lse, row_lse, logits, mine, other)
    own, one0, two0 = make_grad(3, 1, 192, *common)
    other_part = image_product(True, scale, of_lane, far, near, own, text_pieces)[0]
    got = swapped(other_part, "dp", 1)
    of_lane, image_own, to1, to2, to3 = image_product(
        False, scale, of_lane, far, near, own, text_pieces, got
    )
    image_in = [image_own, moved_x(to1, 1), moved_x(to3, 3), moved_x(to2, 2)]
    one_left = after(one_left, image_own)
    of_tower, *ends = end_sums(
        of_tower, one_far_left, one_far_right, one0, two0, one_left, one_right, two_left, two_right
    )
    one_in = [ends[0], moved_z(ends[1], 1), moved_z(ends[3], -1), moved_z(ends[2], 2)]
    two_in = [ends[4], moved_y(ends[5], 1), moved_y(ends[7], -1), moved_y(ends[6], 2)]
    image_own = after(image_own, ends[0])
    image_out, of_lane = image_backward(
        flag, of_lane, image_own, *image_in[1:], *image_parts[1:], image_gain, image_projection
    )
    one_own_sum = after(one_in[0], image_out)
    text_out, loss = text_backward(
        of_tower, of_lane, one_own_sum, *one_in[1:], *two_in, *text_parts, text_gain, text_projection
    )
    text_out = collected(text_out, z, y)
    return (image_out[None, None], text_out[None, None], loss[0, :1] / 12288)


def solution(mesh):
    in_specs = (P("tower", "dp", None, None), P("tower", "dp", None, None), P(), P(), P(), P(), P())
    out_specs = (P("tower", "dp", None, None), P("tower", "dp", None, None), P())
    return jax.shard_map(local, mesh=mesh, in_specs=in_specs, out_specs=out_specs, check_vma=False)
```

```python
import functools

import jax
import jax.numpy as jnp
import numpy as np
from jax import lax
from jax.experimental import pallas as pl
from jax.experimental.pallas import tpu as pltpu
from jax.sharding import PartitionSpec as P

bf = jnp.bfloat16
f32 = jnp.float32
epsilon_norm = 1e-05
epsilon_unit = 1e-06
lowest = -1e30


def moved_z(a, step):
    pairs = [(z * 4 + y, (z + step) % 4 * 4 + y) for z in range(4) for y in range(4)]
    return lax.ppermute(a, "tower", pairs)


def moved_y(a, step):
    pairs = [(z * 4 + y, z * 4 + (y + step) % 4) for z in range(4) for y in range(4)]
    return lax.ppermute(a, "tower", pairs)


def moved_x(a, step):
    pairs = [(x * 2 + c, (x + step) % 4 * 2 + c) for x in range(4) for c in range(2)]
    return lax.ppermute(a, "dp", pairs)


def swapped(a, axis, bit):
    count = lax.axis_size(axis)
    return lax.ppermute(a, axis, [(i, i ^ bit) for i in range(count)])


def after(value, *earlier):
    return lax.optimization_barrier((value, *earlier))[0]


def near_far(a, move):
    return {0: a, 1: move(a, -1), 3: move(a, 1), 2: move(a, 2)}


def in_order(parts):
    return jnp.concatenate([parts[k] for k in range(4)], 0)


def spread(rows):
    count = rows.shape[0] // 4
    return [
        lax.ppermute(rows[q * count : (q + 1) * count], "tower", [(12 + k, q * 4 + k) for k in range(4)])
        for q in range(3)
    ]


def collected(part):
    return [lax.ppermute(part, "tower", [(q * 4 + k, 12 + k) for k in range(4)]) for q in range(3)]


pieces = 16
piece_rows = 96
small_cost = pl.CostEstimate(flops=1000, bytes_accessed=1000, transcendentals=0)
place_one = {2: 0, 1: 2, 3: 3, 0: 6}
place_two = {2: 1, 1: 4, 3: 5, 0: 7}
params = pltpu.CompilerParams(vmem_limit_bytes=28 * 1024 * 1024)
whole = pl.BlockSpec(memory_space=pltpu.VMEM)
scalars = pl.BlockSpec(memory_space=pltpu.SMEM)
anywhere = pl.BlockSpec(memory_space=pltpu.HBM)
note_shape = jax.ShapeDtypeStruct((8, 128), f32)


def shaped(rows, width=1280, dtype=bf):
    return jax.ShapeDtypeStruct((rows, width), dtype)


def full(a):
    return pl.BlockSpec(a.shape, lambda i: (0,) * len(a.shape))


def single(kernel, name, outs, args, held=()):
    return pl.pallas_call(
        kernel,
        grid=(1,),
        in_specs=[scalars] * len(held) + [full(a) for a in args],
        out_specs=[full(o) for o in outs],
        out_shape=outs,
        compiler_params=params,
        cost_estimate=small_cost,
        name=name,
    )(*held, *args)


def held(kernel, name, outs, args):
    return pl.pallas_call(
        kernel,
        in_specs=[whole] * len(args),
        out_specs=[whole] * len(outs),
        out_shape=outs,
        compiler_params=params,
        cost_estimate=small_cost,
        name=name,
    )(*args)


def fetch(piece_refs, text, sems):
    copies = []
    for i, ref in enumerate(piece_refs):
        copy = pltpu.make_async_copy(ref, text.at[pl.ds(i * piece_rows, piece_rows)], sems.at[i])
        copy.start()
        copies.append(copy)
    for copy in copies:
        copy.wait()


def logits_kernel(scale, row_base, col_index, mine, other, *refs):
    piece_refs, (logits, row_out, col_out, text_out, text, high, summed, sems) = refs[:pieces], refs[pieces:]
    step = pl.program_id(0)

    @pl.when(step == 0)
    def _():
        fetch(piece_refs, text, sems)
        pltpu.make_async_copy(text, text_out, sems.at[pieces]).start()
        high[...] = jnp.full(high.shape, -3e38, f32)
        summed[...] = jnp.zeros(summed.shape, f32)
        row_out[...] = jnp.zeros(row_out.shape, f32)

    rows = jnp.concatenate([mine[...], other[...]], 0)
    tile = lax.dot_general(rows, text[...], (((1,), (1,)), ((), ())), preferred_element_type=f32)
    tile = tile * scale[0] + scale[1]
    logits[0] = tile[:128]
    logits[1] = tile[128:]
    row_high = jnp.max(tile, axis=1, keepdims=True)
    row_lse = row_high + jnp.log(jnp.sum(jnp.exp(tile - row_high), axis=1, keepdims=True))
    for h in range(2):
        across = jnp.transpose(jnp.broadcast_to(row_lse[h * 128 : h * 128 + 128], (128, 128)))
        row_out[pl.ds(4 * h + step, 1), :] = across[:1]
    latest = jnp.maximum(high[...], jnp.max(tile, axis=0, keepdims=True))
    summed[...] = summed[...] * jnp.exp(high[...] - latest) + jnp.sum(
        jnp.exp(tile - latest), axis=0, keepdims=True
    )
    high[...] = latest
    place = lax.broadcasted_iota(jnp.int32, (128, 1536), 0)
    matched = jnp.zeros((1, 1), f32)
    for h in range(2):
        hit = place + row_base[4 * h + step] == col_index[...]
        inside = jnp.where(hit, tile[h * 128 : h * 128 + 128], 0.0)
        matched += jnp.sum(jnp.sum(inside, axis=0, keepdims=True), axis=1, keepdims=True)
    row_out[8:16, :] += jnp.broadcast_to(matched, (8, 128))

    @pl.when(step == 3)
    def _():
        pltpu.make_async_copy(text, text_out, sems.at[pieces]).wait()
        value = high[...] + jnp.log(summed[...])
        for i in range(32):
            col_out[i : i + 1, :] = value[:, 48 * i : 48 * i + 48]


def make_logits(scale, row_base, col_index, mine, other, text_pieces):
    return pl.pallas_call(
        logits_kernel,
        grid=(4,),
        in_specs=[scalars, scalars, pl.BlockSpec((1, 1536), lambda i: (0, 0))]
        + [pl.BlockSpec((128, 1280), lambda i: (i, 0))] * 2
        + [anywhere] * pieces,
        out_specs=[
            pl.BlockSpec((2, 128, 1536), lambda i: (0, i, 0)),
            pl.BlockSpec((16, 128), lambda i: (0, 0)),
            pl.BlockSpec((32, 48), lambda i: (0, 0)),
            anywhere,
        ],
        out_shape=[
            jax.ShapeDtypeStruct((2, 512, 1536), f32),
            jax.ShapeDtypeStruct((16, 128), f32),
            jax.ShapeDtypeStruct((32, 48), f32),
            shaped(1536),
        ],
        scratch_shapes=[
            pltpu.VMEM((1536, 1280), bf),
            pltpu.VMEM((1, 1536), f32),
            pltpu.VMEM((1, 1536), f32),
            pltpu.SemaphoreType.DMA((pieces + 1,)),
        ],
        compiler_params=params,
        cost_estimate=small_cost,
        name="logits",
    )(scale, row_base, col_index, mine, other, *text_pieces)


def ring_sum(values):
    return (values[0] + values[2]) + (values[1] + values[3])


def joined(parts):
    highest = parts[0]
    for part in parts[1:]:
        highest = jnp.maximum(highest, part)
    terms = [jnp.exp(part - highest) for part in parts]
    return highest + jnp.log(ring_sum(terms) if len(terms) == 4 else terms[0] + terms[1])


def join_cols(by_block, own, got):
    rows, sums = {}, {}
    for half, place in enumerate((place_one, place_two)):
        for k in range(4):
            for j in range(4):
                row = 4 * place[k] + j
                parts = [own[row : row + 1, :]]
                for s in (1, 2, 3):
                    source = 4 * place[(k - s) % 4] + j if by_block[half] else 4 * place[k] + (j - s) % 4
                    parts.append(got[s - 1][source : source + 1, :])
                rows[row] = joined(parts)
                sums[half, k, j] = rows[row]
    return rows, sums


def first_kernel(col, col1, col2, col3, row, row1, row2, row3, col_out, row_out):
    rows, _ = join_cols((False, True), col, (col1, col2, col3))
    for i, value in rows.items():
        col_out[i : i + 1, :] = value
    got = (row1, row2, row3)
    for h in range(2):
        for k in range(4):
            at = 4 * h + k
            parts = [row[at : at + 1, :]]
            for s in (1, 2, 3):
                source = 4 * h + (k - s) % 4
                parts.append(got[s - 1][source : source + 1, :])
            row_out[at : at + 1, :] = joined(parts)
    row_out[8:16, :] = ring_sum([row[8:16, :], row1[8:16, :], row2[8:16, :], row3[8:16, :]])


def second_kernel(is_image, col, col1, col2, col3, row, row_got, col_out, row_out, of_lane, of_tower):
    rows, sums = join_cols((True, False), col, (col1, col2, col3))
    for i, value in rows.items():
        col_out[:, 48 * i : 48 * i + 48] = value
    halves = [
        ring_sum([ring_sum([sums[half, k, j] for j in range(4)]) for k in range(4)]) for half in range(2)
    ]
    of_cols = jnp.sum(halves[0] + halves[1], axis=1, keepdims=True)
    of_lane[...] = jnp.broadcast_to(0.5 * of_cols, (8, 128))
    values = {}
    for h in range(2):
        for k in range(4):
            at, source = 4 * h + k, 4 * (1 - h) + k
            value = joined([row[at : at + 1, :], row_got[source : source + 1, :]])
            row_out[at : at + 1, :] = value
            values[h, k] = value
    pair = [ring_sum([values[h, k] for k in range(4)]) for h in range(2)]
    of_rows = jnp.sum(pair[0] + pair[1], axis=1, keepdims=True)
    matched = row[8:16, :] + row_got[8:16, :]
    share = 0.5 * jnp.broadcast_to(of_rows, (8, 128)) - matched
    of_tower[...] = jnp.where(is_image[0] > 0, share, 0.0)


def statistics(is_image, col, row):
    col_got = [moved_z(col, -s) for s in (1, 2, 3)]
    row_got = [moved_x(row, -s) for s in (1, 2, 3)]
    col_got, row_got = lax.optimization_barrier((col_got, row_got))
    outs = [jax.ShapeDtypeStruct((32, 48), f32), jax.ShapeDtypeStruct((16, 128), f32)]
    col, row = single(first_kernel, "first_merge", outs, [col, *col_got, row, *row_got])
    col_got = [moved_y(col, -s) for s in (1, 2, 3)]
    row_got = swapped(row, "dp", 1)
    col_got, row_got = lax.optimization_barrier((col_got, row_got))
    outs = [jax.ShapeDtypeStruct((1, 1536), f32), jax.ShapeDtypeStruct((8, 128), f32), note_shape, note_shape]
    return single(second_kernel, "second_merge", outs, [col, *col_got, row, row_got], [is_image])


def write_note(out, at, note):
    value = note[:1, :]
    high = value.astype(bf).astype(f32)
    middle = (value - high).astype(bf).astype(f32)
    low = value - high - middle
    lane = lax.broadcasted_iota(jnp.int32, (1, 128), 1)
    terms = jnp.where(lane == 0, high, jnp.where(lane == 1, middle, jnp.where(lane == 2, low, 0.0)))
    out[at : at + 16, :128] = jnp.broadcast_to(terms, (16, 128)).astype(bf)


def read_note(ref, at):
    terms = ref[at : at + 16, :128].astype(f32)[:1, :]
    lane = lax.broadcasted_iota(jnp.int32, (1, 128), 1)
    total = jnp.sum(jnp.where(lane < 3, terms, 0.0), axis=1, keepdims=True)
    return jnp.broadcast_to(total, (8, 128))


def grad_kernel(steps, rows_out, noted, scale, row_base, col_index, col_lse, row_lse, logits, mine, other, *refs):
    if noted:
        note, refs = refs[0], refs[1:]
    grad, outs, across = refs[0], refs[1:-1], refs[-1]
    step = pl.program_id(0)

    @pl.when(step == 0)
    def _():
        for r in range(8):
            across[r] = jnp.transpose(jnp.broadcast_to(row_lse[r : r + 1, :], (128, 128)))

    place = lax.broadcasted_iota(jnp.int32, (128, 384), 0)
    for r in range(8):
        h, k = r // 4, r % 4
        tile = logits[h, k * 128 : k * 128 + 128, :]
        of_row = jnp.concatenate([across[r]] * 3, 1)
        value = 0.5 * (jnp.exp(tile - of_row) + jnp.exp(tile - col_lse[...]))
        value = jnp.where(place + row_base[r] == col_index[...], value - 1.0, value)
        grad[h, k * 128 : k * 128 + 128, :] = value.astype(bf)
    dims = (((0,), (0,)), ((), ()))
    product = lax.dot_general(grad[0], mine[...], dims, preferred_element_type=f32)
    product += lax.dot_general(grad[1], other[...], dims, preferred_element_type=f32)
    product = (product * scale[0]).astype(bf)
    each = len(outs) // steps
    for s in range(steps):

        def store(s=s):
            for i in range(each):
                outs[s * each + i][:rows_out, :] = product[i * rows_out : i * rows_out + rows_out]

        if steps > 1:
            pl.when(step == s)(store)
        else:
            store()
    if noted:
        for out in outs[:2]:
            out[rows_out:, :] = jnp.zeros((16, 1280), bf)
            write_note(out, rows_out, note)


def make_grad(offset, steps, rows_out, scale, row_base, col_index, col_lse, row_lse, logits, mine, other, note=None):
    count = steps * 384 // rows_out
    outs = [shaped(rows_out + 16 if note is not None and i < 2 else rows_out) for i in range(count)]
    extra = [] if note is None else [note]
    return pl.pallas_call(
        functools.partial(grad_kernel, steps, rows_out, note is not None),
        grid=(steps,),
        in_specs=[scalars, scalars]
        + [pl.BlockSpec((1, 384), lambda i: (0, offset + i))] * 2
        + [full(row_lse), pl.BlockSpec((2, 512, 384), lambda i: (0, 0, offset + i)), full(mine), full(other)]
        + [full(e) for e in extra],
        out_specs=[pl.BlockSpec((2, 512, 384), lambda i: (0, 0, i))] + [full(o) for o in outs],
        out_shape=[jax.ShapeDtypeStruct((2, 512, 384 * steps), bf)] + outs,
        scratch_shapes=[pltpu.VMEM((8, 128, 128), f32)],
        compiler_params=params,
        cost_estimate=small_cost,
        name="text_product",
    )(scale, row_base, col_index, col_lse, row_lse, logits, mine, other, *extra)


def near_kernel(one1, one3, two1, two3, one_left, one_right, two_left, two_right, *outs):
    a, b, c, d = outs
    add = lambda x, y: (x.astype(f32) + y.astype(f32)).astype(bf)
    a[:96] = add(one1[:96], one_left[:96])
    a[96:192] = one1[96:]
    a[192:208] = jnp.zeros((16, 1280), bf)
    write_note(a, 192, read_note(one_left, 96))
    b[:96] = one3[:96]
    b[96:192] = add(one3[96:], one_right[:96])
    c[:96] = add(two1[:96], two_left[...])
    c[96:192] = two1[96:]
    d[:96] = two3[:96]
    d[96:192] = add(two3[96:], two_right[...])


def near_sums(*args):
    outs = [shaped(208), shaped(192), shaped(192), shaped(192)]
    return held(near_kernel, "near_sums", outs, args)


def end_kernel(note, one_left_far, one_right_far, one0, two0, one_left, one_right, two_left, two_right, total_note, *outs):
    three = lambda a, b, c: (a.astype(f32) + b.astype(f32) + c.astype(f32)).astype(bf)
    value = ring_sum([note[...], read_note(one_right_far, 96), read_note(one_left, 192), read_note(one_left_far, 96)])
    total_note[...] = value
    for k in range(4):
        cut = slice(k * 48, k * 48 + 48)
        outs[k][:48, :] = three(one0[cut, :], one_left[cut, :], one_right[cut, :])
        if k:
            outs[k][48:, :] = jnp.zeros((16, 1280), bf)
            write_note(outs[k], 48, value)
        outs[4 + k][...] = three(two0[cut, :], two_left[cut, :], two_right[cut, :])


def end_sums(*args):
    outs = [note_shape, shaped(48), shaped(64), shaped(64), shaped(64)] + [shaped(48)] * 4
    return held(end_kernel, "end_sums", outs, args)


def image_kernel(first, scale, note, far, near, own, text, *refs):
    if first:
        (out,) = refs
    else:
        got, total_note, *outs = refs
        value = note[...] + read_note(got, 512)
        total_note[...] = value
    for k in range(4):
        cut = slice(k * 128, k * 128 + 128)
        rows = jnp.concatenate([far[0, cut, :], near[0, cut, :], own[0, cut, :]], 1)
        product = jnp.dot(rows, text[...], preferred_element_type=f32) * scale[0]
        if first:
            out[cut, :] = product.astype(bf)
        else:
            product = (product + got[cut, :].astype(f32)).astype(bf)
            if k != 2:
                outs[k][...] = product
            else:
                for out, piece in ((outs[2], product[:64]), (outs[4], product[64:])):
                    out[:64, :] = piece
                    out[64:, :] = jnp.zeros((16, 1280), bf)
                    write_note(out, 64, value)
    if first:
        out[512:, :] = jnp.zeros((16, 1280), bf)
        write_note(out, 512, note)


def image_product(first, scale, note, far, near, own, text, got=None):
    outs = [shaped(528)] if first else [note_shape, shaped(128), shaped(128), shaped(80), shaped(128), shaped(80)]
    half = lambda a: pl.BlockSpec((1,) + a.shape[1:], lambda i: (1 if first else 0, 0, 0))
    extra = [] if first else [got]
    return pl.pallas_call(
        functools.partial(image_kernel, first),
        grid=(1,),
        in_specs=[scalars, full(note), half(far), half(near), half(own), full(text)] + [full(e) for e in extra],
        out_specs=[full(o) for o in outs],
        out_shape=outs,
        compiler_params=params,
        cost_estimate=small_cost,
        name="image_product",
    )(scale, note, far, near, own, text, *extra)


def image_near_kernel(right, left, got_left, got_right, to_right, to_left):
    add = lambda x, y: (x.astype(f32) + y.astype(f32)).astype(bf)
    to_right[:64, :] = add(right[:64], got_left[:64])
    to_right[64:128, :] = right[64:]
    to_right[128:, :] = jnp.zeros((16, 1280), bf)
    write_note(to_right, 128, read_note(got_left, 64))
    to_left[:64, :] = left[:64]
    to_left[64:, :] = add(left[64:], got_right[:64])


def backward_rows(grad_unit, unit_exact, length, normal_rows, inverse, gain, projection):
    dot_along = jnp.sum(unit_exact * grad_unit, axis=1, keepdims=True)
    grad_projected = ((grad_unit - unit_exact * dot_along) / length).astype(bf)
    grad_normed = lax.dot_general(
        grad_projected, projection, (((1,), (1,)), ((), ())), preferred_element_type=f32
    )
    scaled = grad_normed * gain
    centre = jnp.mean(scaled, axis=1, keepdims=True)
    tilt_mean = jnp.mean(scaled * normal_rows, axis=1, keepdims=True)
    return inverse * (scaled - centre - normal_rows * tilt_mean)


def image_back_kernel(
    is_image, note, tower, own, left, right, far_left, far_right, unit, length, normal, inverse, gain, projection, out, total
):
    of_lane = ring_sum([note[...], read_note(far_right, 64), read_note(left, 128), read_note(far_left, 64)])
    total[...] = tower[...] + of_lane
    rows = lambda ref: ref[:128, :].astype(f32)
    grad_unit = rows(own) + rows(left) + rows(right)
    value = backward_rows(
        grad_unit, unit[...], length[...], normal[...], inverse[...], gain[...], projection[...]
    )
    out[...] = jnp.where(is_image[0] > 0, value, 0.0).astype(bf)


def image_backward(is_image, *args):
    return single(image_back_kernel, "image_backward", [shaped(128, 1664), note_shape], args, [is_image])


def text_back_kernel(tower, a0, a1, a3, a2, b0, b1, b3, b2, unit, length, normal, inverse, gain, projection, out, total):
    total[...] = ring_sum([tower[...], read_note(a3, 48), read_note(a2, 48), read_note(a1, 48)])
    rows = lambda ref: ref[:48, :].astype(f32)
    one = (rows(a0) + rows(a2)) + (rows(a1) + rows(a3))
    two = (rows(b0) + rows(b2)) + (rows(b1) + rows(b3))
    value = backward_rows(
        jnp.concatenate([one, two], 0),
        unit[...], length[...], normal[...], inverse[...], gain[...], projection[...],
    )
    out[...] = value.astype(bf)


def text_backward(*args):
    return single(text_back_kernel, "text_backward", [shaped(96), note_shape], args)


def forward_kernel(cuts, keep, rows, gain, projection, *outs):
    values = rows[...].astype(f32)
    centred = values - jnp.mean(values, axis=1, keepdims=True)
    inverse = lax.rsqrt(jnp.mean(centred * centred, axis=1, keepdims=True) + epsilon_norm)
    normal = centred * inverse
    normed = (normal * gain[...]).astype(bf)
    projected = jnp.dot(normed, projection[...], preferred_element_type=f32)
    length = jnp.sqrt(jnp.sum(projected * projected, axis=1, keepdims=True) + epsilon_unit)
    unit = projected / length
    rounded = jnp.where(keep[0] > 0, unit, 0.0).astype(bf)
    each = rounded.shape[0] // cuts
    for i in range(cuts):
        outs[i][...] = rounded[i * each : i * each + each]
    unit_out, length_out, normal_out, inverse_out = outs[cuts:]
    unit_out[...] = unit
    length_out[...] = length
    normal_out[...] = normal
    inverse_out[...] = inverse


def forward_tower(cuts, keep, rows, gain, projection):
    count, width = rows.shape
    outs = [shaped(count // cuts)] * cuts + [
        shaped(count, 1280, f32), shaped(count, 1, f32), shaped(count, width, f32), shaped(count, 1, f32)
    ]
    return single(functools.partial(forward_kernel, cuts), "forward", outs, [rows, gain, projection], [keep])


def column_tables():
    of_y, of_z, inside = [], [], []
    for place, half in ((2, 0), (2, 1), (1, 0), (3, 0), (1, 1), (3, 1), (0, 0), (0, 1)):
        for j in range(4):
            for r in range(48):
                of_y.append(j if half else place)
                of_z.append(place if half else j)
                inside.append(48 * half + r)
    return [np.array(a, np.int32)[None, :] for a in (of_y, of_z, inside)]


def local(
    image_hidden, text_hidden, image_gain, text_gain, image_projection, text_projection, logit_scale
):
    tower_at = lax.axis_index("tower")
    lane_at = lax.axis_index("dp")
    z, y, x, c = tower_at // 4, tower_at % 4, lane_at // 2, lane_at % 2
    is_image = z < 3
    flag = jnp.reshape(is_image.astype(jnp.int32), (1,))
    image_rows = image_hidden[0, 0]
    text_got = spread(text_hidden[0, 0])
    scale = jnp.concatenate([logit_scale, jnp.reshape(jnp.where(is_image, 0.0, lowest), (1,))])
    of_y, of_z, inside = column_tables()
    col_index = lane_at * 1536 + (y + of_y) % 4 * 384 + (z + of_z) % 4 * 96 + inside
    steps = np.array([0, 1, 2, 3] * 2, np.int32)
    core = np.array([0] * 4 + [1] * 4, np.int32)
    row_base = tower_at * 1024 + (2 * ((x + steps) % 4) + (c + core) % 2) * 128
    row_base = jnp.where(is_image, row_base, -(1 << 20))

    every = jnp.ones((1,), jnp.int32)
    image_gain, text_gain = image_gain[None, :], text_gain[None, :]
    image_parts = forward_tower(1, flag, image_rows, image_gain, image_projection)
    text_got, image_unit = lax.optimization_barrier((text_got, image_parts[0]))
    text_rows = jnp.where(z == 3, text_hidden[0, 0, 288:], text_got[0] + text_got[1] + text_got[2])
    image_left, image_right = moved_x(image_unit, 1), moved_x(image_unit, -1)
    one_unit, two_unit, *text_parts = forward_tower(2, every, text_rows, text_gain, text_projection)
    one, two = near_far(one_unit, moved_z), near_far(two_unit, moved_y)
    one, two, image_left, image_right = lax.optimization_barrier((one, two, image_left, image_right))
    image_far = [moved_x(image_left[:64], 1), moved_x(image_right[64:], -1)]
    one_low = jnp.concatenate([one[0], one[1]], 0)
    two_low = jnp.concatenate([two[0], two[1]], 0)
    one_high = jnp.concatenate([one[2], one[3]], 0)
    two_high = jnp.concatenate([two[2], two[3]], 0)
    passed = [moved_y(one_low, 1), moved_y(one_high, -1), moved_z(two_low, 1), moved_z(two_high, -1)]
    mine = jnp.concatenate([image_unit, image_right, *image_far, image_left], 0)
    passed, mine, scale, row_base, col_index = lax.optimization_barrier(
        (passed, mine, scale, row_base, col_index)
    )
    other = swapped(mine, "dp", 1)
    far = [moved_y(passed[0], 1), moved_y(passed[1], -1), moved_z(passed[2], 1), moved_z(passed[3], -1)]
    kept = [moved_y(one_low, -1), moved_y(one_high, 1), moved_z(two_low, -1), moved_z(two_high, 1)]
    far, kept, other = lax.optimization_barrier((far, kept, other))
    text_pieces = far + [
        kept[0], passed[1], passed[0], kept[1], kept[2], passed[3], passed[2], kept[3],
        one_low, one_high, two_low, two_high,
    ]

    logits, row_part, col_part, text = make_logits(scale, row_base, col_index, mine, other, text_pieces)
    col_lse, row_lse, of_lane, of_tower = statistics(flag, col_part, row_part)

    common = (scale, row_base, col_index, col_lse, row_lse, logits, mine, other)
    far, one_a, one_b, two_a, two_b = make_grad(0, 1, 96, *common, note=of_tower)
    far_in = [moved_y(one_a, 1), moved_y(one_b, -1), moved_z(two_a, 1), moved_z(two_b, -1)]
    near, *near_parts = make_grad(1, 2, 192, *common)
    far_in, near = lax.optimization_barrier((far_in, near))
    sent = near_sums(*near_parts, *far_in)
    row_lse = after(row_lse, sent[0])
    common = (scale, row_base, col_index, col_lse, row_lse, logits, mine, other)
    own, one0, two0 = make_grad(3, 1, 192, *common)
    other_part = image_product(True, scale, of_lane, far, near, own, text)[0]
    sent, own = lax.optimization_barrier((sent, own))
    near_in = [moved_y(sent[0], 1), moved_y(sent[1], -1), moved_z(sent[2], 1), moved_z(sent[3], -1)]
    near_in, other_part = lax.optimization_barrier((near_in, other_part))
    got = swapped(other_part, "dp", 1)
    of_tower, *ends = end_sums(of_tower, far_in[0], far_in[1], one0, two0, *near_in)
    one_in = [ends[0], moved_z(ends[1], 1), moved_z(ends[3], -1), moved_z(ends[2], 2)]
    two_in = [ends[4], moved_y(ends[5], 1), moved_y(ends[7], -1), moved_y(ends[6], 2)]
    got = after(got, ends[0])
    of_lane, image_own, to_right, far_low, to_left, far_high = image_product(
        False, scale, of_lane, far, near, own, text, got
    )
    far_in = [moved_x(far_low, 1), moved_x(far_high, -1)]
    one_in, two_in, far_in = lax.optimization_barrier((one_in, two_in, far_in))
    to_right, to_left = held(
        image_near_kernel, "image_near", [shaped(144), shaped(128)], [to_right, to_left, *far_in]
    )
    image_in = [image_own, moved_x(to_right, 1), moved_x(to_left, -1), *far_in]
    text_parts = after(text_parts, to_right)
    text_out, of_tower = text_backward(of_tower, *one_in, *two_in, *text_parts, text_gain, text_projection)
    image_in = after(image_in, text_out)
    image_out, loss = image_backward(
        flag, of_lane, of_tower, *image_in, *image_parts[1:], image_gain, image_projection
    )
    text_got, image_out = lax.optimization_barrier((collected(text_out), image_out))
    text_out = jnp.concatenate(text_got + [jnp.where(z == 3, text_out, jnp.zeros_like(text_out))], 0)
    return (image_out[None, None], text_out[None, None], loss[0, :1] / 12288)


def solution(mesh):
    in_specs = (P("tower", "dp", None, None), P("tower", "dp", None, None), P(), P(), P(), P(), P())
    out_specs = (P("tower", "dp", None, None), P("tower", "dp", None, None), P())
    return jax.shard_map(local, mesh=mesh, in_specs=in_specs, out_specs=out_specs, check_vma=False)
```

```python
import functools

import jax
import jax.numpy as jnp
import numpy as np
from jax import lax
from jax.experimental import pallas as pl
from jax.experimental.pallas import tpu as pltpu
from jax.sharding import PartitionSpec as P

bf = jnp.bfloat16
f32 = jnp.float32
epsilon_norm = 1e-05
epsilon_unit = 1e-06
lowest = -1e30


def moved_z(a, step):
    pairs = [(z * 4 + y, (z + step) % 4 * 4 + y) for z in range(4) for y in range(4)]
    return lax.ppermute(a, "tower", pairs)


def moved_y(a, step):
    pairs = [(z * 4 + y, z * 4 + (y + step) % 4) for z in range(4) for y in range(4)]
    return lax.ppermute(a, "tower", pairs)


def moved_x(a, step):
    pairs = [(x * 2 + c, (x + step) % 4 * 2 + c) for x in range(4) for c in range(2)]
    return lax.ppermute(a, "dp", pairs)


def swapped(a, axis, bit):
    count = lax.axis_size(axis)
    return lax.ppermute(a, axis, [(i, i ^ bit) for i in range(count)])


def after(value, *earlier):
    return lax.optimization_barrier((value, *earlier))[0]


def near_far(a, move):
    return {0: a, 1: move(a, -1), 3: move(a, 1), 2: move(a, 2)}


def in_order(parts):
    return jnp.concatenate([parts[k] for k in range(4)], 0)


def spread(rows):
    count = rows.shape[0] // 4
    return [
        lax.ppermute(rows[q * count : (q + 1) * count], "tower", [(12 + k, q * 4 + k) for k in range(4)])
        for q in range(3)
    ]


def collected(part):
    return [lax.ppermute(part, "tower", [(q * 4 + k, 12 + k) for k in range(4)]) for q in range(3)]


pieces = 16
piece_rows = 96
small_cost = pl.CostEstimate(flops=1000, bytes_accessed=1000, transcendentals=0)
place_one = {2: 0, 1: 2, 3: 3, 0: 6}
place_two = {2: 1, 1: 4, 3: 5, 0: 7}
params = pltpu.CompilerParams(vmem_limit_bytes=28 * 1024 * 1024)
whole = pl.BlockSpec(memory_space=pltpu.VMEM)
scalars = pl.BlockSpec(memory_space=pltpu.SMEM)
anywhere = pl.BlockSpec(memory_space=pl.ANY)
in_hbm = pl.BlockSpec(memory_space=pltpu.HBM)
note_shape = jax.ShapeDtypeStruct((8, 128), f32)


def shaped(rows, width=1280, dtype=bf):
    return jax.ShapeDtypeStruct((rows, width), dtype)


def full(a):
    return pl.BlockSpec(a.shape, lambda i: (0,) * len(a.shape))


def single(kernel, name, outs, args, held=()):
    return pl.pallas_call(
        kernel,
        grid=(1,),
        in_specs=[scalars] * len(held) + [full(a) for a in args],
        out_specs=[full(o) for o in outs],
        out_shape=outs,
        compiler_params=params,
        cost_estimate=small_cost,
        name=name,
    )(*held, *args)


def held(kernel, name, outs, args):
    return pl.pallas_call(
        kernel,
        in_specs=[whole] * len(args),
        out_specs=[whole] * len(outs),
        out_shape=outs,
        compiler_params=params,
        cost_estimate=small_cost,
        name=name,
    )(*args)


def fetch(piece_refs, text, sems):
    copies = []
    for i, ref in enumerate(piece_refs):
        copy = pltpu.make_async_copy(ref, text.at[pl.ds(i * piece_rows, piece_rows)], sems.at[i])
        copy.start()
        copies.append(copy)
    for copy in copies:
        copy.wait()


def logits_kernel(scale, row_base, col_index, mine, other, *refs):
    piece_refs, (logits, row_out, col_out, text_out, text, high, summed, sems) = refs[:pieces], refs[pieces:]
    step = pl.program_id(0)

    @pl.when(step == 0)
    def _():
        fetch(piece_refs, text, sems)
        pltpu.make_async_copy(text, text_out, sems.at[pieces]).start()
        high[...] = jnp.full(high.shape, -3e38, f32)
        summed[...] = jnp.zeros(summed.shape, f32)
        row_out[...] = jnp.zeros(row_out.shape, f32)

    rows = jnp.concatenate([mine[...], other[...]], 0)
    tile = lax.dot_general(rows, text[...], (((1,), (1,)), ((), ())), preferred_element_type=f32)
    tile = tile * scale[0] + scale[1]
    logits[0] = tile[:128]
    logits[1] = tile[128:]
    row_high = jnp.max(tile, axis=1, keepdims=True)
    row_lse = row_high + jnp.log(jnp.sum(jnp.exp(tile - row_high), axis=1, keepdims=True))
    for h in range(2):
        across = jnp.transpose(jnp.broadcast_to(row_lse[h * 128 : h * 128 + 128], (128, 128)))
        row_out[pl.ds(4 * h + step, 1), :] = across[:1]
    latest = jnp.maximum(high[...], jnp.max(tile, axis=0, keepdims=True))
    summed[...] = summed[...] * jnp.exp(high[...] - latest) + jnp.sum(
        jnp.exp(tile - latest), axis=0, keepdims=True
    )
    high[...] = latest
    place = lax.broadcasted_iota(jnp.int32, (128, 1536), 0)
    matched = jnp.zeros((1, 1), f32)
    for h in range(2):
        hit = place + row_base[4 * h + step] == col_index[...]
        inside = jnp.where(hit, tile[h * 128 : h * 128 + 128], 0.0)
        matched += jnp.sum(jnp.sum(inside, axis=0, keepdims=True), axis=1, keepdims=True)
    row_out[8:16, :] += jnp.broadcast_to(matched, (8, 128))

    @pl.when(step == 3)
    def _():
        pltpu.make_async_copy(text, text_out, sems.at[pieces]).wait()
        value = high[...] + jnp.log(summed[...])
        for i in range(32):
            col_out[i : i + 1, :] = value[:, 48 * i : 48 * i + 48]


def make_logits(scale, row_base, col_index, mine, other, text_pieces):
    return pl.pallas_call(
        logits_kernel,
        grid=(4,),
        in_specs=[scalars, scalars, pl.BlockSpec((1, 1536), lambda i: (0, 0))]
        + [pl.BlockSpec((128, 1280), lambda i: (i, 0))] * 2
        + [in_hbm] * 12
        + [anywhere] * 4,
        out_specs=[
            pl.BlockSpec((2, 128, 1536), lambda i: (0, i, 0)),
            pl.BlockSpec((16, 128), lambda i: (0, 0)),
            pl.BlockSpec((32, 48), lambda i: (0, 0)),
            anywhere,
        ],
        out_shape=[
            jax.ShapeDtypeStruct((2, 512, 1536), f32),
            jax.ShapeDtypeStruct((16, 128), f32),
            jax.ShapeDtypeStruct((32, 48), f32),
            shaped(1536),
        ],
        scratch_shapes=[
            pltpu.VMEM((1536, 1280), bf),
            pltpu.VMEM((1, 1536), f32),
            pltpu.VMEM((1, 1536), f32),
            pltpu.SemaphoreType.DMA((pieces + 1,)),
        ],
        compiler_params=params,
        cost_estimate=small_cost,
        name="logits",
    )(scale, row_base, col_index, mine, other, *text_pieces)


def pack_kernel(a0, a1, a2, a3, b0, b1, b2, b3, a_low, a_high, b_low, b_high):
    for first, second, out in ((a0, a1, a_low), (a2, a3, a_high), (b0, b1, b_low), (b2, b3, b_high)):
        out[:48, :] = first[...]
        out[48:, :] = second[...]


def ring_sum(values):
    return (values[0] + values[2]) + (values[1] + values[3])


def joined(parts):
    highest = parts[0]
    for part in parts[1:]:
        highest = jnp.maximum(highest, part)
    terms = [jnp.exp(part - highest) for part in parts]
    return highest + jnp.log(ring_sum(terms) if len(terms) == 4 else terms[0] + terms[1])


def join_cols(by_block, own, got):
    rows, sums = {}, {}
    for half, place in enumerate((place_one, place_two)):
        for k in range(4):
            for j in range(4):
                row = 4 * place[k] + j
                parts = [own[row : row + 1, :]]
                for s in (1, 2, 3):
                    source = 4 * place[(k - s) % 4] + j if by_block[half] else 4 * place[k] + (j - s) % 4
                    parts.append(got[s - 1][source : source + 1, :])
                rows[row] = joined(parts)
                sums[half, k, j] = rows[row]
    return rows, sums


def first_kernel(col, col1, col2, col3, row, row1, row2, row3, col_out, row_out):
    rows, _ = join_cols((False, True), col, (col1, col2, col3))
    for i, value in rows.items():
        col_out[i : i + 1, :] = value
    got = (row1, row2, row3)
    for h in range(2):
        for k in range(4):
            at = 4 * h + k
            parts = [row[at : at + 1, :]]
            for s in (1, 2, 3):
                source = 4 * h + (k - s) % 4
                parts.append(got[s - 1][source : source + 1, :])
            row_out[at : at + 1, :] = joined(parts)
    row_out[8:16, :] = ring_sum([row[8:16, :], row1[8:16, :], row2[8:16, :], row3[8:16, :]])


def second_kernel(is_image, col, col1, col2, col3, row, row_got, col_out, row_out, of_lane, of_tower):
    rows, sums = join_cols((True, False), col, (col1, col2, col3))
    for i, value in rows.items():
        col_out[:, 48 * i : 48 * i + 48] = value
    halves = [
        ring_sum([ring_sum([sums[half, k, j] for j in range(4)]) for k in range(4)]) for half in range(2)
    ]
    of_cols = jnp.sum(halves[0] + halves[1], axis=1, keepdims=True)
    of_lane[...] = jnp.broadcast_to(0.5 * of_cols, (8, 128))
    values = {}
    for h in range(2):
        for k in range(4):
            at, source = 4 * h + k, 4 * (1 - h) + k
            value = joined([row[at : at + 1, :], row_got[source : source + 1, :]])
            row_out[at : at + 1, :] = value
            values[h, k] = value
    pair = [ring_sum([values[h, k] for k in range(4)]) for h in range(2)]
    of_rows = jnp.sum(pair[0] + pair[1], axis=1, keepdims=True)
    matched = row[8:16, :] + row_got[8:16, :]
    share = 0.5 * jnp.broadcast_to(of_rows, (8, 128)) - matched
    of_tower[...] = jnp.where(is_image[0] > 0, share, 0.0)


def statistics(is_image, col, row):
    col_got = [moved_z(col, -s) for s in (1, 2, 3)]
    row_got = [moved_x(row, -s) for s in (1, 2, 3)]
    col_got, row_got = lax.optimization_barrier((col_got, row_got))
    outs = [jax.ShapeDtypeStruct((32, 48), f32), jax.ShapeDtypeStruct((16, 128), f32)]
    col, row = single(first_kernel, "first_merge", outs, [col, *col_got, row, *row_got])
    col_got = [moved_y(col, -s) for s in (1, 2, 3)]
    row_got = swapped(row, "dp", 1)
    col_got, row_got = lax.optimization_barrier((col_got, row_got))
    outs = [jax.ShapeDtypeStruct((1, 1536), f32), jax.ShapeDtypeStruct((8, 128), f32), note_shape, note_shape]
    return single(second_kernel, "second_merge", outs, [col, *col_got, row, row_got], [is_image])


def write_note(out, at, note):
    value = note[:1, :]
    high = value.astype(bf).astype(f32)
    middle = (value - high).astype(bf).astype(f32)
    low = value - high - middle
    lane = lax.broadcasted_iota(jnp.int32, (1, 128), 1)
    terms = jnp.where(lane == 0, high, jnp.where(lane == 1, middle, jnp.where(lane == 2, low, 0.0)))
    out[at : at + 16, :128] = jnp.broadcast_to(terms, (16, 128)).astype(bf)


def read_note(ref, at):
    terms = ref[at : at + 16, :128].astype(f32)[:1, :]
    lane = lax.broadcasted_iota(jnp.int32, (1, 128), 1)
    total = jnp.sum(jnp.where(lane < 3, terms, 0.0), axis=1, keepdims=True)
    return jnp.broadcast_to(total, (8, 128))


def grad_kernel(steps, rows_out, noted, scale, row_base, col_index, col_lse, row_lse, logits, mine, other, *refs):
    if noted:
        note, refs = refs[0], refs[1:]
    grad, outs, across = refs[0], refs[1:-1], refs[-1]
    step = pl.program_id(0)

    @pl.when(step == 0)
    def _():
        for r in range(8):
            across[r] = jnp.transpose(jnp.broadcast_to(row_lse[r : r + 1, :], (128, 128)))

    place = lax.broadcasted_iota(jnp.int32, (128, 384), 0)
    for r in range(8):
        h, k = r // 4, r % 4
        tile = logits[h, k * 128 : k * 128 + 128, :]
        of_row = jnp.concatenate([across[r]] * 3, 1)
        value = 0.5 * (jnp.exp(tile - of_row) + jnp.exp(tile - col_lse[...]))
        value = jnp.where(place + row_base[r] == col_index[...], value - 1.0, value)
        grad[h, k * 128 : k * 128 + 128, :] = value.astype(bf)
    dims = (((0,), (0,)), ((), ()))
    product = lax.dot_general(grad[0], mine[...], dims, preferred_element_type=f32)
    product += lax.dot_general(grad[1], other[...], dims, preferred_element_type=f32)
    product = (product * scale[0]).astype(bf)
    each = len(outs) // steps
    for s in range(steps):

        def store(s=s):
            for i in range(each):
                outs[s * each + i][:rows_out, :] = product[i * rows_out : i * rows_out + rows_out]

        if steps > 1:
            pl.when(step == s)(store)
        else:
            store()
    if noted:
        for out in outs[:2]:
            out[rows_out:, :] = jnp.zeros((16, 1280), bf)
            write_note(out, rows_out, note)


def make_grad(offset, steps, rows_out, scale, row_base, col_index, col_lse, row_lse, logits, mine, other, note=None):
    count = steps * 384 // rows_out
    outs = [shaped(rows_out + 16 if note is not None and i < 2 else rows_out) for i in range(count)]
    extra = [] if note is None else [note]
    return pl.pallas_call(
        functools.partial(grad_kernel, steps, rows_out, note is not None),
        grid=(steps,),
        in_specs=[scalars, scalars]
        + [pl.BlockSpec((1, 384), lambda i: (0, offset + i))] * 2
        + [full(row_lse), pl.BlockSpec((2, 512, 384), lambda i: (0, 0, offset + i)), full(mine), full(other)]
        + [full(e) for e in extra],
        out_specs=[pl.BlockSpec((2, 512, 384), lambda i: (0, 0, i))] + [full(o) for o in outs],
        out_shape=[jax.ShapeDtypeStruct((2, 512, 384 * steps), bf)] + outs,
        scratch_shapes=[pltpu.VMEM((8, 128, 128), f32)],
        compiler_params=params,
        cost_estimate=small_cost,
        name="text_product",
    )(scale, row_base, col_index, col_lse, row_lse, logits, mine, other, *extra)


def near_kernel(one1, one3, two1, two3, one_left, one_right, two_left, two_right, *outs):
    a, b, c, d = outs
    add = lambda x, y: (x.astype(f32) + y.astype(f32)).astype(bf)
    a[:96] = add(one1[:96], one_left[:96])
    a[96:192] = one1[96:]
    a[192:208] = jnp.zeros((16, 1280), bf)
    write_note(a, 192, read_note(one_left, 96))
    b[:96] = one3[:96]
    b[96:192] = add(one3[96:], one_right[:96])
    c[:96] = add(two1[:96], two_left[...])
    c[96:192] = two1[96:]
    d[:96] = two3[:96]
    d[96:192] = add(two3[96:], two_right[...])


def near_sums(*args):
    outs = [shaped(208), shaped(192), shaped(192), shaped(192)]
    return held(near_kernel, "near_sums", outs, args)


def end_kernel(note, one_left_far, one_right_far, one0, two0, one_left, one_right, two_left, two_right, total_note, *outs):
    three = lambda a, b, c: (a.astype(f32) + b.astype(f32) + c.astype(f32)).astype(bf)
    value = ring_sum([note[...], read_note(one_right_far, 96), read_note(one_left, 192), read_note(one_left_far, 96)])
    total_note[...] = value
    for k in range(4):
        cut = slice(k * 48, k * 48 + 48)
        outs[k][:48, :] = three(one0[cut, :], one_left[cut, :], one_right[cut, :])
        if k:
            outs[k][48:, :] = jnp.zeros((16, 1280), bf)
            write_note(outs[k], 48, value)
        outs[4 + k][...] = three(two0[cut, :], two_left[cut, :], two_right[cut, :])


def end_sums(*args):
    outs = [note_shape, shaped(48), shaped(64), shaped(64), shaped(64)] + [shaped(48)] * 4
    return held(end_kernel, "end_sums", outs, args)


def image_kernel(first, scale, note, far, near, own, text, *refs):
    if first:
        (out,) = refs
    else:
        got, total_note, *outs = refs
        value = note[...] + read_note(got, 512)
        total_note[...] = value
    for k in range(4):
        cut = slice(k * 128, k * 128 + 128)
        rows = jnp.concatenate([far[0, cut, :], near[0, cut, :], own[0, cut, :]], 1)
        product = jnp.dot(rows, text[...], preferred_element_type=f32) * scale[0]
        if first:
            out[cut, :] = product.astype(bf)
        else:
            product = (product + got[cut, :].astype(f32)).astype(bf)
            if k != 2:
                outs[k][...] = product
            else:
                for out, piece in ((outs[2], product[:64]), (outs[4], product[64:])):
                    out[:64, :] = piece
                    out[64:, :] = jnp.zeros((16, 1280), bf)
                    write_note(out, 64, value)
    if first:
        out[512:, :] = jnp.zeros((16, 1280), bf)
        write_note(out, 512, note)


def image_product(first, scale, note, far, near, own, text, got=None):
    outs = [shaped(528)] if first else [note_shape, shaped(128), shaped(128), shaped(80), shaped(128), shaped(80)]
    half = lambda a: pl.BlockSpec((1,) + a.shape[1:], lambda i: (1 if first else 0, 0, 0))
    extra = [] if first else [got]
    return pl.pallas_call(
        functools.partial(image_kernel, first),
        grid=(1,),
        in_specs=[scalars, full(note), half(far), half(near), half(own), full(text)] + [full(e) for e in extra],
        out_specs=[full(o) for o in outs],
        out_shape=outs,
        compiler_params=params,
        cost_estimate=small_cost,
        name="image_product",
    )(scale, note, far, near, own, text, *extra)


def image_near_kernel(right, left, got_left, got_right, to_right, to_left):
    add = lambda x, y: (x.astype(f32) + y.astype(f32)).astype(bf)
    to_right[:64, :] = add(right[:64], got_left[:64])
    to_right[64:128, :] = right[64:]
    to_right[128:, :] = jnp.zeros((16, 1280), bf)
    write_note(to_right, 128, read_note(got_left, 64))
    to_left[:64, :] = left[:64]
    to_left[64:, :] = add(left[64:], got_right[:64])


def backward_rows(grad_unit, unit_exact, length, normal_rows, inverse, gain, projection):
    dot_along = jnp.sum(unit_exact * grad_unit, axis=1, keepdims=True)
    grad_projected = ((grad_unit - unit_exact * dot_along) / length).astype(bf)
    grad_normed = lax.dot_general(
        grad_projected, projection, (((1,), (1,)), ((), ())), preferred_element_type=f32
    )
    scaled = grad_normed * gain
    centre = jnp.mean(scaled, axis=1, keepdims=True)
    tilt_mean = jnp.mean(scaled * normal_rows, axis=1, keepdims=True)
    return inverse * (scaled - centre - normal_rows * tilt_mean)


def image_back_kernel(
    is_image, note, tower, own, left, right, far_left, far_right, unit, length, normal, inverse, gain, projection, out, total
):
    of_lane = ring_sum([note[...], read_note(far_right, 64), read_note(left, 128), read_note(far_left, 64)])
    total[...] = tower[...] + of_lane
    rows = lambda ref: ref[:128, :].astype(f32)
    grad_unit = rows(own) + rows(left) + rows(right)
    value = backward_rows(
        grad_unit, unit[...], length[...], normal[...], inverse[...], gain[...], projection[...]
    )
    out[...] = jnp.where(is_image[0] > 0, value, 0.0).astype(bf)


def image_backward(is_image, *args):
    return single(image_back_kernel, "image_backward", [shaped(128, 1664), note_shape], args, [is_image])


def text_back_kernel(tower, a0, a1, a3, a2, b0, b1, b3, b2, unit, length, normal, inverse, gain, projection, out, total):
    total[...] = ring_sum([tower[...], read_note(a3, 48), read_note(a2, 48), read_note(a1, 48)])
    rows = lambda ref: ref[:48, :].astype(f32)
    one = (rows(a0) + rows(a2)) + (rows(a1) + rows(a3))
    two = (rows(b0) + rows(b2)) + (rows(b1) + rows(b3))
    value = backward_rows(
        jnp.concatenate([one, two], 0),
        unit[...], length[...], normal[...], inverse[...], gain[...], projection[...],
    )
    out[...] = value.astype(bf)


def text_backward(*args):
    return single(text_back_kernel, "text_backward", [shaped(96), note_shape], args)


def forward_kernel(cuts, keep, rows, gain, projection, *outs):
    values = rows[...].astype(f32)
    centred = values - jnp.mean(values, axis=1, keepdims=True)
    inverse = lax.rsqrt(jnp.mean(centred * centred, axis=1, keepdims=True) + epsilon_norm)
    normal = centred * inverse
    normed = (normal * gain[...]).astype(bf)
    projected = jnp.dot(normed, projection[...], preferred_element_type=f32)
    length = jnp.sqrt(jnp.sum(projected * projected, axis=1, keepdims=True) + epsilon_unit)
    unit = projected / length
    rounded = jnp.where(keep[0] > 0, unit, 0.0).astype(bf)
    each = rounded.shape[0] // cuts
    for i in range(cuts):
        outs[i][...] = rounded[i * each : i * each + each]
    unit_out, length_out, normal_out, inverse_out = outs[cuts:]
    unit_out[...] = unit
    length_out[...] = length
    normal_out[...] = normal
    inverse_out[...] = inverse


def forward_tower(cuts, keep, rows, gain, projection):
    count, width = rows.shape
    outs = [shaped(count // cuts)] * cuts + [
        shaped(count, 1280, f32), shaped(count, 1, f32), shaped(count, width, f32), shaped(count, 1, f32)
    ]
    return single(functools.partial(forward_kernel, cuts), "forward", outs, [rows, gain, projection], [keep])


def column_tables():
    of_y, of_z, inside = [], [], []
    for place, half in ((2, 0), (2, 1), (1, 0), (3, 0), (1, 1), (3, 1), (0, 0), (0, 1)):
        for j in range(4):
            for r in range(48):
                of_y.append(j if half else place)
                of_z.append(place if half else j)
                inside.append(48 * half + r)
    return [np.array(a, np.int32)[None, :] for a in (of_y, of_z, inside)]


def local(
    image_hidden, text_hidden, image_gain, text_gain, image_projection, text_projection, logit_scale
):
    tower_at = lax.axis_index("tower")
    lane_at = lax.axis_index("dp")
    z, y, x, c = tower_at // 4, tower_at % 4, lane_at // 2, lane_at % 2
    is_image = z < 3
    flag = jnp.reshape(is_image.astype(jnp.int32), (1,))
    image_rows = image_hidden[0, 0]
    text_got = spread(text_hidden[0, 0])
    scale = jnp.concatenate([logit_scale, jnp.reshape(jnp.where(is_image, 0.0, lowest), (1,))])
    of_y, of_z, inside = column_tables()
    col_index = lane_at * 1536 + (y + of_y) % 4 * 384 + (z + of_z) % 4 * 96 + inside
    steps = np.array([0, 1, 2, 3] * 2, np.int32)
    core = np.array([0] * 4 + [1] * 4, np.int32)
    row_base = tower_at * 1024 + (2 * ((x + steps) % 4) + (c + core) % 2) * 128
    row_base = jnp.where(is_image, row_base, -(1 << 20))

    every = jnp.ones((1,), jnp.int32)
    image_gain, text_gain = image_gain[None, :], text_gain[None, :]
    image_parts = forward_tower(1, flag, image_rows, image_gain, image_projection)
    text_got, image_unit = lax.optimization_barrier((text_got, image_parts[0]))
    text_rows = jnp.where(z == 3, text_hidden[0, 0, 288:], text_got[0] + text_got[1] + text_got[2])
    image_left, image_right = moved_x(image_unit, 1), moved_x(image_unit, -1)
    one_unit, two_unit, *text_parts = forward_tower(2, every, text_rows, text_gain, text_projection)
    one, two = near_far(one_unit, moved_z), near_far(two_unit, moved_y)
    one, two, image_left, image_right = lax.optimization_barrier((one, two, image_left, image_right))
    image_far = [moved_x(image_left[:64], 1), moved_x(image_right[64:], -1)]
    one_low, one_high, two_low, two_high = held(
        pack_kernel, "pack", [shaped(96)] * 4, [part[k] for part in (one, two) for k in range(4)]
    )
    passed = [moved_y(one_low, 1), moved_y(one_high, -1), moved_z(two_low, 1), moved_z(two_high, -1)]
    mine = jnp.concatenate([image_unit, image_right, *image_far, image_left], 0)
    passed, mine, scale, row_base, col_index = lax.optimization_barrier(
        (passed, mine, scale, row_base, col_index)
    )
    other = swapped(mine, "dp", 1)
    far = [moved_y(passed[0], 1), moved_y(passed[1], -1), moved_z(passed[2], 1), moved_z(passed[3], -1)]
    kept = [moved_y(one_low, -1), moved_y(one_high, 1), moved_z(two_low, -1), moved_z(two_high, 1)]
    far, kept, other = lax.optimization_barrier((far, kept, other))
    text_pieces = far + [
        kept[0], passed[1], passed[0], kept[1], kept[2], passed[3], passed[2], kept[3],
        one_low, one_high, two_low, two_high,
    ]

    logits, row_part, col_part, text = make_logits(scale, row_base, col_index, mine, other, text_pieces)
    col_lse, row_lse, of_lane, of_tower = statistics(flag, col_part, row_part)

    common = (scale, row_base, col_index, col_lse, row_lse, logits, mine, other)
    far, one_a, one_b, two_a, two_b = make_grad(0, 1, 96, *common, note=of_tower)
    far_in = [moved_y(one_a, 1), moved_y(one_b, -1), moved_z(two_a, 1), moved_z(two_b, -1)]
    near, *near_parts = make_grad(1, 2, 192, *common)
    far_in, near = lax.optimization_barrier((far_in, near))
    sent = near_sums(*near_parts, *far_in)
    row_lse = after(row_lse, sent[0])
    common = (scale, row_base, col_index, col_lse, row_lse, logits, mine, other)
    own, one0, two0 = make_grad(3, 1, 192, *common)
    other_part = image_product(True, scale, of_lane, far, near, own, text)[0]
    sent, own = lax.optimization_barrier((sent, own))
    near_in = [moved_y(sent[0], 1), moved_y(sent[1], -1), moved_z(sent[2], 1), moved_z(sent[3], -1)]
    near_in, other_part = lax.optimization_barrier((near_in, other_part))
    got = swapped(other_part, "dp", 1)
    of_tower, *ends = end_sums(of_tower, far_in[0], far_in[1], one0, two0, *near_in)
    one_in = [ends[0], moved_z(ends[1], 1), moved_z(ends[3], -1), moved_z(ends[2], 2)]
    two_in = [ends[4], moved_y(ends[5], 1), moved_y(ends[7], -1), moved_y(ends[6], 2)]
    got = after(got, ends[0])
    of_lane, image_own, to_right, far_low, to_left, far_high = image_product(
        False, scale, of_lane, far, near, own, text, got
    )
    far_in = [moved_x(far_low, 1), moved_x(far_high, -1)]
    one_in, two_in, far_in = lax.optimization_barrier((one_in, two_in, far_in))
    to_right, to_left = held(
        image_near_kernel, "image_near", [shaped(144), shaped(128)], [to_right, to_left, *far_in]
    )
    image_in = [image_own, moved_x(to_right, 1), moved_x(to_left, -1), *far_in]
    text_parts = after(text_parts, to_right)
    text_out, of_tower = text_backward(of_tower, *one_in, *two_in, *text_parts, text_gain, text_projection)
    image_in = after(image_in, text_out)
    image_out, loss = image_backward(
        flag, of_lane, of_tower, *image_in, *image_parts[1:], image_gain, image_projection
    )
    text_got, image_out = lax.optimization_barrier((collected(text_out), image_out))
    text_out = jnp.concatenate(text_got + [jnp.where(z == 3, text_out, jnp.zeros_like(text_out))], 0)
    return (image_out[None, None], text_out[None, None], loss[0, :1] / 12288)


def solution(mesh):
    in_specs = (P("tower", "dp", None, None), P("tower", "dp", None, None), P(), P(), P(), P(), P())
    out_specs = (P("tower", "dp", None, None), P("tower", "dp", None, None), P())
    return jax.shard_map(local, mesh=mesh, in_specs=in_specs, out_specs=out_specs, check_vma=False)
```
